32 devices in a mesh: fsdp: 4 (over y, x), expert: 4 (over z), tensor: 2 (over core).
Axes of the slice: x: 2, y: 2, z: 4, core: 2. Of those that a mesh axis runs over, the one named last changes fastest.
Arguments:
- tokens: bfloat16 [2, 256, 4096], P(None, 'expert'), may hold values from -6 to 6
- route: int32 [2, 256, 2], P(None, 'expert'), may hold values from 0 to 7, all different within a row; in each aligned block of 64 rows (0 to 63, 64 to 127, ..., all dimensions but the last counted through in order) at most 32 rows name the same one
- route_weight: float32 [2, 256, 2], P(None, 'expert'), may hold values from 0.1 to 1
- gate_up: bfloat16 [8, 2, 4096, 8192], P('expert', None, None, ('fsdp', 'tensor')), may hold values from -0.09375 to 0.09375
- down_weight: bfloat16 [8, 8192, 4096], P('expert', ('fsdp', 'tensor')), may hold values from -0.09375 to 0.09375
- adam_first: float32 [8, 2048, 4096], P(None, ('fsdp', 'tensor'), 'expert'), may hold values from -2.5 to 2.5
- adam_second: float32 [8, 2048, 4096], P(None, ('fsdp', 'tensor'), 'expert'), may hold values from 0.05 to 1
- gradient: bfloat16 [8, 2048, 4096], P(None, ('fsdp', 'tensor'), 'expert'), may hold values from -6 to 6
- block_list: int32 [8, 8, 4], P(None, ('fsdp', 'tensor')), may hold values from 0 to 31, as said below
- block_count: int32 [8, 8], P(None, ('fsdp', 'tensor')), may hold values from 1 to 4, as said below
Outputs:
- mixed: bfloat16 [2, 256, 4096], P(None, 'expert', ('fsdp', 'tensor'))
- first_new: float32 [8, 2048, 4096], P(None, ('fsdp', 'tensor'), 'expert')
- second_new: float32 [8, 2048, 4096], P(None, ('fsdp', 'tensor'), 'expert')
The draws below stay inside these ranges and needn't reach their ends.
Inputs may be any that keep to these rules, and one draw needn't show every extreme that they name: `route`: the two experts of a token differ; in each aligned block of 64 tokens of one step no expert is named more than 32 times. `block_list`: the 4 entries of one list are distinct block numbers; only the first block_count entries are applied. `block_count`: 4 is reached in every draw.
All inputs are finite; a program needn't handle non-finite values.
Results may differ from the reference program's by a relative error of at most 0.023.
Values may be sent and summed in bfloat16 or wider, within the bound.
No kernel may reach another device: no remote copies, remote signals or barrier semaphores. Data moves between devices by JAX's collectives and lax.ppermute only.
A program may use at most 192 MiB of HBM per device.

```python
import math
import jax
import jax.numpy as jnp
import numpy as np
from jax import lax

D = 4096
HID = 8192
E = 8
STRIDE = 4
BLOCK_ROWS = 8
MAXCH = 4
S = 2
TOK_DEV = 64
TOK = 256
CAP = 32
SHARDS = 8
HSHARD = 1024
BUCKET = 2048
NBLOCKS = 32
N_EXPERT = 4


def draw_block_list(key, part):
    key = jax.random.fold_in(key, 7)
    row_keys = jax.random.split(key, E * SHARDS)
    orders = jax.vmap(lambda row_key: jax.random.permutation(row_key, NBLOCKS))(row_keys)
    return orders[:, :MAXCH].reshape(E, SHARDS, MAXCH).astype(jnp.int32)


def draw_block_count(key, part):
    key = jax.random.fold_in(key, 13)
    key_base, key_busy, key_top = jax.random.split(key, 3)
    base_count = 1 + (jax.random.randint(key_base, (E, SHARDS), 0, 4) == 0).astype(jnp.int32)
    busy_flag = jax.random.randint(key_busy, (E, SHARDS), 0, 16) == 0
    counts = jnp.where(busy_flag, MAXCH, base_count)
    top_index = jax.random.randint(key_top, (), 0, E * SHARDS)
    flat_counts = counts.reshape(-1).at[top_index].set(MAXCH)
    return flat_counts.reshape(E, SHARDS).astype(jnp.int32)


def with_spikes(drawn, rng, source, target, parts, factor):
    owner, partner = [(jnp.arange(drawn.shape[position]) // (drawn.shape[position] // parts)).reshape([-1 if axis == position else 1 for axis in range(drawn.ndim)]) for position in (source, target)]
    chosen = jax.random.permutation(rng, parts)[partner]
    strong = (owner == chosen) | (owner == (partner + parts // 2) % parts)
    return jnp.where(strong, factor * drawn, drawn)


def block_scale(stream_key, dims, cuts, least, top_value):
    loudness = 1.0
    for axis_at, shards_of in cuts:
        draws = jax.random.uniform(jax.random.fold_in(jax.random.fold_in(stream_key, 6), axis_at), (shards_of,), jnp.float32, least / len(cuts), top_value / len(cuts))
        loudness = loudness * jnp.repeat(jnp.exp(draws), dims[axis_at] // shards_of).reshape((-1,) + (1,) * (len(dims) - 1 - axis_at))
    return loudness


def assign_block(key, own, number, rows, number_of, top, bound, slope):
    sequence = jax.random.permutation(key, number_of)
    heavy_load, ordinary = portions_of(number_of, rows * top, bound, slope, True), portions_of(number_of, rows * top, bound, slope, False)
    places = jnp.arange(number_of)

    def named(sizes, rotation):
        used = int((sizes > 0).sum())
        fixed = max(1, used // 4)
        moved = fixed + (places - fixed + rotation * (used - fixed)) % max(1, number_of - fixed)
        return jnp.zeros((number_of,), jnp.int32).at[sequence[jnp.where(places < fixed, places, moved)]].set(jnp.asarray(sizes, jnp.int32))

    sizes = jnp.where(number % 4 == 0, named(heavy_load, number // 4), named(ordinary, number - number // 4 - 1))
    mixed = jax.random.permutation(jax.random.fold_in(own, 3), number_of)
    donor, taker = mixed[0:number_of // 2 * 2:2], mixed[1:number_of // 2 * 2:2]
    room = jnp.minimum(sizes[donor] - 1, bound - sizes[taker]) // 2
    room = jnp.where((donor == sequence[0]) | (taker == sequence[0]) | (sizes[taker] == 0), 0, jnp.maximum(room, 0))
    moved = jax.random.randint(jax.random.fold_in(own, 4), (number_of // 2,), 0, 1 << 20) % (room + 1)
    sizes = sizes.at[donor].add(-moved).at[taker].add(moved)
    members = jnp.searchsorted(jnp.cumsum(sizes), jnp.arange(rows * top), side="right").astype(jnp.int32)
    table = members.reshape(top, rows).T
    table = table[jax.random.permutation(jax.random.fold_in(own, 1), rows)]
    rotation = jax.random.randint(jax.random.fold_in(own, 2), (rows, 1), 0, top)
    return jnp.take_along_axis(table, (jnp.arange(top)[None, :] + rotation) % top, axis=1)


def portions_of(count, total, bound, lean, full):
    weights = [(1 << 20) // math.isqrt(standing ** lean) + 1 for standing in range(1, count + 1)]
    largest = bound if full else min(bound, max(-(-total // count), total * weights[0] // sum(weights)))
    least = 1 if total - largest >= count - 1 else 0
    given, spare = [largest] + [least] * (count - 1), total - largest - least * (count - 1)
    while spare > 0:
        free = [i for i in range(1, count) if given[i] < largest] or [i for i in range(1, count) if given[i] < bound]
        pool, left = sum([weights[i] for i in free]), spare
        for i in free:
            more = min(bound - given[i], max(1, left * weights[i] // pool), spare)
            given[i] = given[i] + more
            spare = spare - more
    return np.array(given)


def bell_draw(rng, extent, deviation, limit, cuts=(), kind=jnp.bfloat16):
    entries = deviation * jax.random.normal(rng, extent, jnp.float32)
    if cuts:
        entries = entries * block_scale(rng, extent, cuts, -0.22, 0.18)
    return jnp.clip(entries, -limit, limit).astype(kind)


def noise_with(stream_key, shape, scale, most, shards, heavy, dtype=jnp.bfloat16):
    values = scale * jax.random.normal(stream_key, shape, jnp.float32)
    if shards:
        values = values * block_scale(stream_key, shape, shards, -0.22, 0.18)
    return jnp.clip(with_spikes(values, jax.random.fold_in(stream_key, 3), *heavy), -most, most).astype(dtype)


def setup_inputs(seed: int = 0) -> dict:
    seeds = jax.random.split(jax.random.key(seed), 11)
    tokens = bell_draw(seeds[0], (S, TOK, D), 1.0, 6.0, ((1, 4),))
    route_keys = jax.random.split(jax.random.fold_in(seeds[1], 1), S * TOK // TOK_DEV)
    route_turns = jax.random.permutation(jax.random.fold_in(seeds[1], 3), S * TOK // TOK_DEV)
    route = jax.vmap(lambda own, number: assign_block(jax.random.fold_in(seeds[1], 2), own, number, TOK_DEV, E, 2, TOK_DEV // 2, 2))(route_keys, route_turns).reshape((S, TOK, 2))
    route_weight = jnp.clip(0.1 + 0.9 * jax.random.uniform(seeds[2], (S, TOK, 2), jnp.float32) ** block_scale(seeds[2], (S, TOK, 2), ((1, 4),), -0.2, 0.2), 0.1, 1.0)
    gate_up = bell_draw(seeds[3], (E, 2, D, HID), D ** -0.5, 0.09375, ((0, 4), (3, 8)))
    down_weight = noise_with(seeds[4], (E, HID, D), HID ** -0.5, 0.09375, ((0, 4), (1, 8)), (1, 2, 8, 2.0))
    adam_first = bell_draw(seeds[5], (E, BUCKET, D), 0.3, 2.5, ((1, 8), (2, 4)), jnp.float32)
    adam_second = jnp.clip(jnp.exp(math.log(1.0) - 2.9957323 * jax.random.uniform(seeds[6], (E, BUCKET, D), jnp.float32) ** block_scale(seeds[6], (E, BUCKET, D), ((1, 8), (2, 4)), -0.2, 0.2)), 0.05, 1.0)
    gradient = bell_draw(seeds[7], (E, BUCKET, D), 1.0, 6.0, ((1, 8), (2, 4)))
    block_list = draw_block_list(jax.random.fold_in(seeds[10], 71), 0)
    block_count = draw_block_count(jax.random.fold_in(seeds[10], 71), 0)
    return {"tokens": tokens, "route": route, "route_weight": route_weight, "gate_up": gate_up, "down_weight": down_weight, "adam_first": adam_first, "adam_second": adam_second, "gradient": gradient, "block_list": block_list, "block_count": block_count}


BETA_ONE = 0.9
BETA_TWO = 0.95
LEARN_RATE = 0.03
ADAM_EPS = 1e-08
FIRST_FIX = 1.0 - 0.9 ** 10
SECOND_FIX = 1.0 - 0.95 ** 10

def adam_moments(adam_first, adam_second, gradient):
    grad_wide = gradient.astype(jnp.float32)
    first_new = BETA_ONE * adam_first + (1.0 - BETA_ONE) * grad_wide
    second_new = BETA_TWO * adam_second + (1.0 - BETA_TWO) * grad_wide * grad_wide
    step_size = LEARN_RATE * (first_new / FIRST_FIX) / (jnp.sqrt(second_new / SECOND_FIX) + ADAM_EPS)
    return (first_new, second_new, (-step_size).astype(jnp.bfloat16))

def updated_down(down_weight, delta, block_list, block_count):
    listed = jnp.arange(MAXCH)[None, None, :] < block_count[:, :, None]
    marked = jnp.any((block_list[:, :, :, None] == jnp.arange(NBLOCKS)[None, None, None, :]) & listed[:, :, :, None], axis=2)
    row_mask = jnp.repeat(marked.reshape(E, SHARDS * NBLOCKS), BLOCK_ROWS, axis=1)
    strided = down_weight.reshape(E, BUCKET, STRIDE, D)
    fresh_rows = (strided[:, :, 0, :].astype(jnp.float32) + jnp.where(row_mask[:, :, None], delta.astype(jnp.float32), 0.0)).astype(jnp.bfloat16)
    return jnp.concatenate([fresh_rows[:, :, None, :], strided[:, :, 1:, :]], axis=2).reshape(E, HID, D)

def expert_rows(token_rows, gate_weights, down_rows):
    gate_value = jnp.dot(token_rows, gate_weights[0], preferred_element_type=jnp.float32)
    up_value = jnp.dot(token_rows, gate_weights[1], preferred_element_type=jnp.float32)
    hidden = (jax.nn.silu(gate_value) * up_value).astype(jnp.bfloat16)

    def add_shard(shard_index, running):
        first_unit = (shard_index * HSHARD).astype(jnp.int32)
        shard_term = jnp.dot(lax.dynamic_slice_in_dim(hidden, first_unit, HSHARD, 1), lax.dynamic_slice_in_dim(down_rows, first_unit, HSHARD, 0), preferred_element_type=jnp.float32)
        rounded = lax.optimization_barrier(shard_term.astype(jnp.bfloat16))
        return running + rounded.astype(jnp.float32)
    return lax.fori_loop(0, SHARDS, add_shard, jnp.zeros((token_rows.shape[0], D), jnp.float32))

def reference(tokens, route, route_weight, gate_up, down_weight, adam_first, adam_second, gradient, block_list, block_count):
    first_new, second_new, delta = adam_moments(adam_first, adam_second, gradient)
    down_new = updated_down(down_weight, delta, block_list, block_count)
    flat_tokens = tokens.reshape(S * TOK, D)
    flat_route = route.reshape(-1)
    flat_weight = route_weight.reshape(-1)
    owner_token = (jnp.arange(S * TOK * 2) // 2).astype(jnp.int32)
    capacity_all = S * N_EXPERT * CAP
    combined = jnp.zeros((S * TOK, D), jnp.float32)
    for expert in range(E):
        chosen = flat_route == expert
        picked = jnp.nonzero(chosen, size=capacity_all, fill_value=0)[0].astype(jnp.int32)
        live_slot = jnp.arange(capacity_all) < jnp.sum(chosen.astype(jnp.int32))
        token_index = owner_token[picked]
        result = expert_rows(flat_tokens[token_index], gate_up[expert], down_new[expert])
        pair_weight = jnp.where(live_slot, flat_weight[picked], 0.0)
        combined = combined.at[token_index].add(pair_weight[:, None] * result)
    return (combined.reshape(S, TOK, D).astype(jnp.bfloat16), first_new, second_new)
```

```python
import functools

import jax
import jax.numpy as jnp
from jax import lax
from jax.experimental import pallas as pl
from jax.experimental.pallas import tpu as pltpu
from jax.sharding import PartitionSpec as P

STRIDE = 4
BLOCK_ROWS = 8
MAXCH = 4
CAP = 32
HALF = 256
UNIT_TILE = 512

BETA_ONE = 0.9
BETA_TWO = 0.95
LEARN_RATE = 0.03
ADAM_EPS = 1e-08
FIRST_FIX = 1.0 - 0.9**10
SECOND_FIX = 1.0 - 0.95**10

F32 = jnp.float32
BF16 = jnp.bfloat16
SMALL_VMEM = 16 * 2**20
STAGE_VMEM = 24 * 2**20


def adam_kernel(list_ref, count_ref, first_ref, second_ref, grad_ref, first_out, second_out, delta_out):
    expert = pl.program_id(0)
    grad = grad_ref[...].astype(F32)
    first_out[...] = BETA_ONE * first_ref[...] + (1.0 - BETA_ONE) * grad
    second_out[...] = BETA_TWO * second_ref[...] + (1.0 - BETA_TWO) * grad * grad
    parts = []
    for entry in range(MAXCH):
        start = pl.multiple_of(list_ref[expert * MAXCH + entry] * BLOCK_ROWS, BLOCK_ROWS)
        first = first_out[0, pl.ds(start, BLOCK_ROWS), :]
        second = second_out[0, pl.ds(start, BLOCK_ROWS), :]
        step = LEARN_RATE * (first / FIRST_FIX) / (jnp.sqrt(second / SECOND_FIX) + ADAM_EPS)
        parts.append(jnp.where(entry < count_ref[expert], -step, 0.0))
    delta_out[0] = jnp.concatenate(parts, axis=0).astype(BF16)


def adam_update(adam_first, adam_second, gradient, block_list, block_count):
    experts, rows, cols = adam_first.shape
    block = pl.BlockSpec((1, rows, cols), lambda e, *_: (e, 0, 0))
    size = experts * rows * cols
    return pl.pallas_call(
        adam_kernel,
        grid_spec=pltpu.PrefetchScalarGridSpec(
            num_scalar_prefetch=2,
            grid=(experts,),
            in_specs=[block, block, block],
            out_specs=[block, block, pl.BlockSpec((1, MAXCH * BLOCK_ROWS, cols), lambda e, *_: (e, 0, 0))],
        ),
        out_shape=[
            jax.ShapeDtypeStruct(adam_first.shape, F32),
            jax.ShapeDtypeStruct(adam_first.shape, F32),
            jax.ShapeDtypeStruct((experts, MAXCH * BLOCK_ROWS, cols), BF16),
        ],
        compiler_params=pltpu.CompilerParams(vmem_limit_bytes=SMALL_VMEM),
        cost_estimate=pl.CostEstimate(flops=8 * size, bytes_accessed=18 * size, transcendentals=0),
        name="adam_listed",
    )(block_list, block_count, adam_first, adam_second, gradient)


def route_kernel(groups, owned, tok_block, meta_ref, *refs):
    infos = refs[:groups]
    select_ref, scatter_ref, weight_ref = refs[groups:]
    halves = scatter_ref.shape[0]
    per_half = groups // halves
    half_slots = (HALF // tok_block) * CAP
    first_expert = (meta_ref[0] * owned).astype(F32)
    row = lax.broadcasted_iota(jnp.int32, (HALF, HALF), 0)
    col = lax.broadcasted_iota(jnp.int32, (HALF, HALF), 1)
    before = ((row < col) & (row // tok_block == col // tok_block)).astype(F32).astype(BF16)
    slot = lax.broadcasted_iota(jnp.int32, (half_slots, HALF), 0)
    token = lax.broadcasted_iota(jnp.int32, (half_slots, HALF), 1)
    same_block = slot // CAP == token // tok_block
    slot_pos = (slot % CAP).astype(F32)
    for half in range(halves):
        info = jnp.concatenate([infos[k][...] for k in range(half * per_half, (half + 1) * per_half)], axis=1)
        selectors = []
        for e in range(owned):
            named = first_expert + e
            hit_a, hit_b = info[0:1] == named, info[1:2] == named
            member = jnp.where(hit_a | hit_b, 1.0, 0.0)
            weight = jnp.where(hit_a, info[2:3], 0.0) + jnp.where(hit_b, info[3:4], 0.0)
            position = jnp.dot(
                jnp.broadcast_to(member, (16, HALF)).astype(BF16), before, preferred_element_type=F32
            )[0:1]
            chosen = same_block & (position == slot_pos) & (member > 0.5)
            selectors.append(jnp.where(chosen, 1.0, 0.0))
            slot_weight = jnp.sum(jnp.where(chosen, weight, 0.0), axis=1, keepdims=True)
            weight_ref[e, half * half_slots : (half + 1) * half_slots, :] = jnp.broadcast_to(
                slot_weight, (half_slots, 128)
            )
        selector = jnp.concatenate(selectors, axis=0)
        select_ref[half] = selector.astype(BF16)
        scatter_ref[half] = jnp.transpose(selector).astype(BF16)


def route_tables(meta, infos, owned, tok_block):
    groups = len(infos)
    halves = groups * infos[0].shape[1] // HALF
    half_slots = (HALF // tok_block) * CAP
    vmem = pl.BlockSpec(memory_space=pltpu.VMEM)
    return pl.pallas_call(
        functools.partial(route_kernel, groups, owned, tok_block),
        grid_spec=pltpu.PrefetchScalarGridSpec(
            num_scalar_prefetch=1, grid=(), in_specs=[vmem] * groups, out_specs=[vmem] * 3
        ),
        out_shape=[
            jax.ShapeDtypeStruct((halves, owned * half_slots, HALF), BF16),
            jax.ShapeDtypeStruct((halves, HALF, owned * half_slots), BF16),
            jax.ShapeDtypeStruct((owned, halves * half_slots, 128), F32),
        ],
        compiler_params=pltpu.CompilerParams(vmem_limit_bytes=SMALL_VMEM),
        cost_estimate=pl.CostEstimate(flops=10**7, bytes_accessed=10**6, transcendentals=0),
        name="route_tables",
    )(meta, *infos)


def gate_up_kernel(shares, within, first, last, meta_ref, select_ref, weight_ref, tokens_ref, *refs):
    recv = [refs[i * within : (i + 1) * within] for i in range(shares)]
    refs = refs[shares * within :]
    if first:
        gate_up_ref, refs = refs[0], refs[1:]
    else:
        gate_up_ref, sums_ref, refs = refs[0], refs[1], refs[2:]
    out_ref, rows_ref, total_ref = refs
    expert, share = pl.program_id(0), pl.program_id(2)
    steps, tok_block, width = tokens_ref.shape
    cols = recv[0][0].shape[2]
    halves = select_ref.shape[0]
    per_half = HALF // (steps * tok_block)
    owned = rows_ref.shape[1]
    half_slots = select_ref.shape[1] // owned

    @pl.when((expert == 0) & (pl.program_id(1) == 0) & (share == 0))
    def _():
        for i in range(shares):
            for q in range(within):
                place = meta_ref[shares + q]
                start = (meta_ref[i] * within + place) * cols
                lanes = pl.ds(pl.multiple_of(start, cols), cols)
                into = pl.ds(pl.multiple_of(place * cols, cols), cols)
                for half in range(halves):
                    blocks = []
                    for k in range(half * per_half, (half + 1) * per_half):
                        if k == 0:
                            blocks += [tokens_ref[s, :, lanes] for s in range(steps)]
                        else:
                            blocks.append(recv[i][q][k - 1])
                    picked = jnp.dot(
                        select_ref[half], jnp.concatenate(blocks, axis=0), preferred_element_type=F32
                    ).astype(BF16)
                    for e in range(owned):
                        rows_ref[i, e, half * half_slots : (half + 1) * half_slots, into] = picked[
                            e * half_slots : (e + 1) * half_slots
                        ]

    rows = rows_ref[share, expert]
    gate = jnp.dot(rows, gate_up_ref[0, 0], preferred_element_type=F32)
    up = jnp.dot(rows, gate_up_ref[0, 1], preferred_element_type=F32)

    def finish(gate, up):
        if last:
            out_ref[0] = (gate * jax.nn.sigmoid(gate) * up * weight_ref[expert, :, 0:1]).astype(BF16)
        else:
            out_ref[0, 0], out_ref[0, 1] = gate, up

    if shares == 1:
        if not first:
            gate, up = gate + sums_ref[0, 0], up + sums_ref[0, 1]
        finish(gate, up)
    else:

        @pl.when(share == 0)
        def _():
            total_ref[0] = gate if first else gate + sums_ref[0, 0]
            total_ref[1] = up if first else up + sums_ref[0, 1]

        @pl.when((share > 0) & (share < shares - 1))
        def _():
            total_ref[0] += gate
            total_ref[1] += up

        @pl.when(share == shares - 1)
        def _():
            finish(total_ref[0] + gate, total_ref[1] + up)


def gate_up_stage(places, select, weight, tokens, received, gate_up, sums, last):
    owned, _, width, units = gate_up.shape
    shares, within = len(received), len(received[0])
    depth = within * received[0][0].shape[2]
    slots = weight.shape[1]
    tile = min(UNIT_TILE, units)
    vmem = pl.BlockSpec(memory_space=pltpu.VMEM)
    sums_spec = pl.BlockSpec((1, 2, slots, tile), lambda e, j, i, *_: (e, 0, 0, j))
    if last:
        out_spec = pl.BlockSpec((1, slots, tile), lambda e, j, i, *_: (e, 0, j))
        out_shape = jax.ShapeDtypeStruct((owned, slots, units), BF16)
    else:
        out_spec = sums_spec
        out_shape = jax.ShapeDtypeStruct((owned, 2, slots, units), F32)
    first = sums is None
    return pl.pallas_call(
        functools.partial(gate_up_kernel, shares, within, first, last),
        grid_spec=pltpu.PrefetchScalarGridSpec(
            num_scalar_prefetch=1,
            grid=(owned, units // tile, shares),
            in_specs=[vmem] * (3 + shares * within)
            + [pl.BlockSpec((1, 2, depth, tile), lambda e, j, i, meta: (e, 0, meta[i], j))]
            + ([] if first else [sums_spec]),
            out_specs=out_spec,
            scratch_shapes=[
                pltpu.VMEM((shares, owned, slots, depth), BF16),
                pltpu.VMEM((2, slots, tile), F32),
            ],
        ),
        out_shape=out_shape,
        compiler_params=pltpu.CompilerParams(vmem_limit_bytes=STAGE_VMEM),
        cost_estimate=pl.CostEstimate(
            flops=4 * owned * slots * depth * units * shares,
            bytes_accessed=4 * owned * depth * units * shares + 16 * owned * slots * units,
            transcendentals=0,
        ),
        name="gate_up_stage",
    )(places, select, weight, tokens, *sum([list(r) for r in received], []), gate_up, *([] if first else [sums]))


def down_kernel(owned, within, meta_ref, list_ref, hidden_ref, scatter_ref, delta_ref, down_ref, *refs):
    outs, (buf, sem) = refs[:within], refs[within:]
    cols = buf.shape[3]
    src_cols = delta_ref.shape[3]
    halves = scatter_ref.shape[0]
    half_slots = hidden_ref.shape[1] // halves
    order = list(range(1, within)) + [0]

    def fetch(q, e):
        lanes = pl.ds(pl.multiple_of(meta_ref[1 + q] * cols, cols), cols)
        return pltpu.make_async_copy(down_ref.at[e, :, lanes], buf.at[q, e], sem.at[q, e])

    for q in order:
        for e in range(owned):
            fetch(q, e).start()
    listed = MAXCH * BLOCK_ROWS
    span = BLOCK_ROWS * STRIDE
    row = lax.broadcasted_iota(jnp.int32, (MAXCH * span, listed), 0)
    col = lax.broadcasted_iota(jnp.int32, (MAXCH * span, listed), 1)
    spread = ((row // STRIDE == col) & (row % STRIDE == 0)).astype(F32).astype(BF16)
    for q in order:
        first_col = meta_ref[1 + q] * cols
        source = first_col // src_cols
        lanes = pl.ds(pl.multiple_of(first_col - source * src_cols, cols), cols)
        parts = []
        for e in range(owned):
            added = jnp.dot(spread, delta_ref[source, e, :, lanes], preferred_element_type=F32)
            fetch(q, e).wait()
            for entry in range(MAXCH):
                block = list_ref[(meta_ref[0] * owned + e) * MAXCH + entry]
                where = pl.ds(pl.multiple_of(block * span, span), span)
                fresh = buf[q, e, where, :].astype(F32) + added[entry * span : (entry + 1) * span]
                buf[q, e, where, :] = fresh.astype(BF16)
            parts.append(jnp.dot(hidden_ref[e], buf[q, e], preferred_element_type=F32).astype(BF16))
        for half in range(halves):
            mine = jnp.concatenate([p[half * half_slots : (half + 1) * half_slots] for p in parts], axis=0)
            outs[q][half * HALF : (half + 1) * HALF, :] = jnp.dot(
                scatter_ref[half], mine, preferred_element_type=F32
            ).astype(BF16)


def down_pieces(meta, block_list, hidden, scatter, delta, down_weight, cols):
    owned, units, _ = down_weight.shape
    within = meta.shape[0] - 1
    rows = scatter.shape[0] * HALF
    slots = hidden.shape[1]
    vmem = pl.BlockSpec(memory_space=pltpu.VMEM)
    return pl.pallas_call(
        functools.partial(down_kernel, owned, within),
        grid_spec=pltpu.PrefetchScalarGridSpec(
            num_scalar_prefetch=2,
            grid=(),
            in_specs=[vmem, vmem, vmem, pl.BlockSpec(memory_space=pl.ANY)],
            out_specs=[vmem] * within,
            scratch_shapes=[
                pltpu.VMEM((within, owned, units, cols), BF16),
                pltpu.SemaphoreType.DMA((within, owned)),
            ],
        ),
        out_shape=[jax.ShapeDtypeStruct((rows, cols), BF16)] * within,
        compiler_params=pltpu.CompilerParams(vmem_limit_bytes=STAGE_VMEM),
        cost_estimate=pl.CostEstimate(
            flops=2 * owned * slots * units * cols * within,
            bytes_accessed=2 * owned * units * cols * within,
            transcendentals=0,
        ),
        name="down_mixed",
    )(meta, block_list, hidden, scatter, delta, down_weight)


def swap(value, axis, distance):
    return lax.ppermute(value, axis, [(i, i ^ distance) for i in range(lax.axis_size(axis))])


def shift(value, axis, distance):
    size = lax.axis_size(axis)
    return lax.ppermute(value, axis, [(i, (i + distance) % size) for i in range(size)])


def on_device(
    tokens,
    route,
    route_weight,
    gate_up,
    down_weight,
    adam_first,
    adam_second,
    gradient,
    block_list,
    block_count,
):
    groups = lax.axis_size("expert")
    across, within = lax.axis_size("fsdp"), lax.axis_size("tensor")
    at_z, at_f, at_t = lax.axis_index("expert"), lax.axis_index("fsdp"), lax.axis_index("tensor")
    owned = gate_up.shape[0]
    steps, block, width = tokens.shape
    own_rows = steps * block
    cols = width // (across * within)
    lists = block_list.reshape(-1)
    counts = block_count.reshape(-1)

    share = lax.dynamic_slice_in_dim(tokens, (at_f * within + at_t) * cols, cols, 2).reshape(own_rows, cols)
    info = jnp.concatenate(
        [route.astype(F32).reshape(own_rows, 2).T, route_weight.reshape(own_rows, 2).T, jnp.zeros((4, own_rows), F32)]
    )
    infos = [info] + [shift(info, "expert", k) for k in range(1, groups)]
    away = [shift(share, "expert", k) for k in range(1, groups)]
    first_new, second_new, delta = adam_update(adam_first, adam_second, gradient, lists, counts)
    away, first_new, second_new, delta = lax.optimization_barrier((away, first_new, second_new, delta))
    away = jnp.stack(away)

    here = jnp.stack([at_z]).astype(jnp.int32)
    select, scatter, weight = route_tables(here, infos, owned, block)
    columns = [away] + [swap(away, "fsdp", r) for r in range(1, across)]

    def stage(shares, sums, last):
        places = jnp.stack([at_f ^ r for r in shares] + [at_t ^ q for q in range(within)]).astype(jnp.int32)
        received = [[columns[r]] + [swap(columns[r], "tensor", q) for q in range(1, within)] for r in shares]
        return gate_up_stage(places, select, weight, tokens, received, gate_up, sums, last)

    sums = stage([0], None, False)
    delta, sums = lax.optimization_barrier((delta, sums))
    by_owner = delta.reshape(groups, owned, *delta.shape[1:])
    incoming = lax.all_to_all(by_owner, "expert", split_axis=0, concat_axis=0, tiled=True)
    sums = stage(list(range(1, across - 1)), sums, False)
    hidden = stage([across - 1], sums, True)

    def place(r):
        return jnp.stack([at_z] + [(at_f ^ r) * within + (at_t ^ q) for q in range(within)]).astype(jnp.int32)

    def down(where):
        pieces = down_pieces(where, lists, hidden, scatter, incoming, down_weight, cols)
        return pieces[0], [swap(pieces[q], "tensor", q) for q in range(1, within)]

    def add(*terms):
        total = terms[0].astype(F32)
        for term in terms[1:]:
            total = total + term.astype(F32)
        return total.astype(BF16)

    rows = groups * own_rows
    upper, lower = slice(0, rows // 2), slice(rows // 2, rows)

    def summed(pair, at):
        return add(pair[0][at], *[other[at] for other in pair[1]])

    if across == 4:
        far = down(place(3))
        one = down(place(1))
        far_up, far_low = summed(far, upper), summed(far, lower)
        next_place, far_up, far_low = lax.optimization_barrier((place(2), far_up, far_low))
        by_one, by_two = swap(far_up, "fsdp", 1), swap(far_low, "fsdp", 2)
        two = down(next_place)
        one_sum = summed(one, upper)
        next_place, one_sum, one = lax.optimization_barrier((place(0), one_sum, one))
        one_up = swap(one_sum, "fsdp", 1)
        own = down(next_place)
        one_low = swap(add(one[0][lower], *[o[lower] for o in one[1]], by_two), "fsdp", 1)
        two_low = swap(summed(two, lower), "fsdp", 2)
        two_up = swap(add(two[0][upper], *[o[upper] for o in two[1]], by_one), "fsdp", 2)
        total_up = add(own[0][upper], *[o[upper] for o in own[1]], one_up, two_up)
        total_low = add(own[0][lower], *[o[lower] for o in own[1]], one_low, two_low)
        parts = list(total_up.reshape(groups // 2, own_rows, cols)) + list(
            total_low.reshape(groups // 2, own_rows, cols)
        )
    else:
        others = [swap(summed(down(place(r)), slice(0, rows)), "fsdp", r) for r in range(1, across)]
        parts = list(add(summed(down(place(0)), slice(0, rows)), *others).reshape(groups, own_rows, cols))
    mixed = add(parts[0], *[shift(parts[k], "expert", -k) for k in range(1, groups)])
    return (mixed.reshape(steps, block, cols), first_new, second_new)


def solution(mesh):
    return jax.shard_map(
        on_device,
        mesh=mesh,
        in_specs=(
            P(None, "expert", None),
            P(None, "expert", None),
            P(None, "expert", None),
            P("expert", None, None, ("fsdp", "tensor")),
            P("expert", ("fsdp", "tensor"), None),
            P(None, ("fsdp", "tensor"), "expert"),
            P(None, ("fsdp", "tensor"), "expert"),
            P(None, ("fsdp", "tensor"), "expert"),
            P(None, ("fsdp", "tensor"), None),
            P(None, ("fsdp", "tensor")),
        ),
        out_specs=(
            P(None, "expert", ("fsdp", "tensor")),
            P(None, ("fsdp", "tensor"), "expert"),
            P(None, ("fsdp", "tensor"), "expert"),
        ),
        check_vma=False,
    )
```

```python
import functools

import jax
import jax.numpy as jnp
from jax import lax
from jax.experimental import pallas as pl
from jax.experimental.pallas import tpu as pltpu
from jax.sharding import PartitionSpec as P

STRIDE = 4
BLOCK_ROWS = 8
MAXCH = 4
CAP = 32
UNIT_TILE = 512

BETA_ONE = 0.9
BETA_TWO = 0.95
LEARN_RATE = 0.03
ADAM_EPS = 1e-08
FIRST_FIX = 1.0 - 0.9**10
SECOND_FIX = 1.0 - 0.95**10

F32 = jnp.float32
BF16 = jnp.bfloat16
SMALL_VMEM = 16 * 2**20
STAGE_VMEM = 16 * 2**20


def in_hbm(value):
    return pltpu.with_memory_space_constraint(value, pltpu.HBM)


def as_column(ref, k):
    row = jnp.concatenate([ref[s, k : k + 1, :].astype(F32) for s in range(ref.shape[0])], axis=1)
    return jnp.transpose(jnp.broadcast_to(row, (row.shape[1], row.shape[1])))[:, 0:1]


def pack_kernel(groups, owned, meta_ref, tokens_ref, route_ref, *refs):
    sends, (own_ref, pick_ref) = refs[: groups - 1], refs[groups - 1 :]
    steps, block, width = tokens_ref.shape
    rows = steps * block
    cols = sends[0].shape[1]
    per_expert = steps * CAP
    per_group = owned * per_expert
    slots = groups * per_group
    token = lax.broadcasted_iota(jnp.int32, (rows, rows), 0)
    lane = lax.broadcasted_iota(jnp.int32, (rows, rows), 1)
    before = jnp.where((lane < token) & (lane // block == token // block), 1.0, 0.0).astype(BF16)
    named = [as_column(route_ref, k) for k in range(2)]
    lane = lane.astype(F32)
    member = jnp.where((lane == named[0]) | (lane == named[1]), 1.0, 0.0).astype(BF16)
    earlier = jnp.dot(before, member, preferred_element_type=F32)
    slot = lax.broadcasted_iota(jnp.int32, (rows, slots), 1)
    step = lax.broadcasted_iota(jnp.int32, (rows, slots), 0) // block
    group = (meta_ref[0] + slot // per_group) % groups
    expert = (group * owned + slot % per_group // per_expert).astype(F32)
    here = (slot % per_expert // CAP == step)
    spot = (slot % CAP).astype(F32)
    total = jnp.zeros((rows, slots), F32)
    for k in range(2):
        position = jnp.sum(jnp.where(lane == named[k], earlier, 0.0), axis=1, keepdims=True)
        pick = jnp.where((expert == named[k]) & here & (spot == position), 1.0, 0.0)
        pick_ref[k] = pick.astype(BF16)
        total = total + pick
    select = jnp.transpose(total).astype(BF16)
    lanes = pl.ds(pl.multiple_of(meta_ref[meta_ref.shape[0] - 1] * cols, cols), cols)
    share = jnp.concatenate([tokens_ref[s, :, lanes] for s in range(steps)], axis=0)
    for k in range(1, groups):
        sends[k - 1][...] = jnp.dot(
            select[k * per_group : (k + 1) * per_group], share, preferred_element_type=F32
        ).astype(BF16)
    every = jnp.concatenate([tokens_ref[s] for s in range(steps)], axis=0)
    own_ref[...] = jnp.dot(select[:per_group], every, preferred_element_type=F32).astype(BF16)


def pack_slots(meta, tokens, route, groups, owned, cols):
    steps, block, width = tokens.shape
    rows = steps * block
    per_group = owned * steps * CAP
    vmem = pl.BlockSpec(memory_space=pltpu.VMEM)
    return pl.pallas_call(
        functools.partial(pack_kernel, groups, owned),
        grid_spec=pltpu.PrefetchScalarGridSpec(
            num_scalar_prefetch=1, grid=(), in_specs=[vmem, vmem], out_specs=[vmem] * (groups + 1)
        ),
        out_shape=[jax.ShapeDtypeStruct((per_group, cols), BF16)] * (groups - 1)
        + [
            jax.ShapeDtypeStruct((per_group, width), BF16),
            jax.ShapeDtypeStruct((2, rows, groups * per_group), BF16),
        ],
        compiler_params=pltpu.CompilerParams(vmem_limit_bytes=SMALL_VMEM),
        cost_estimate=pl.CostEstimate(flops=10**7, bytes_accessed=4 * rows * width, transcendentals=0),
        name="pack_slots",
    )(meta, tokens, route.transpose(0, 2, 1))


def combine_kernel(pick_ref, weight_ref, *refs):
    out_ref = refs[-1]
    steps, block, _ = out_ref.shape
    rows = jnp.concatenate([ref[...] for ref in refs[:-1]], axis=0)
    total = jnp.zeros((steps * block, out_ref.shape[2]), F32)
    for k in range(2):
        total = total + as_column(weight_ref, k) * jnp.dot(pick_ref[k], rows, preferred_element_type=F32)
    for s in range(steps):
        out_ref[s] = total[s * block : (s + 1) * block].astype(BF16)


def combine_slots(pick, weight, parts):
    steps, block, _ = weight.shape
    cols = parts[0].shape[1]
    vmem = pl.BlockSpec(memory_space=pltpu.VMEM)
    return pl.pallas_call(
        combine_kernel,
        in_specs=[vmem] * (2 + len(parts)),
        out_specs=vmem,
        out_shape=jax.ShapeDtypeStruct((steps, block, cols), BF16),
        compiler_params=pltpu.CompilerParams(vmem_limit_bytes=SMALL_VMEM),
        cost_estimate=pl.CostEstimate(flops=10**7, bytes_accessed=10**6, transcendentals=0),
        name="combine_slots",
    )(pick, weight.transpose(0, 2, 1), *parts)


def delta_kernel(list_ref, count_ref, first_ref, second_ref, grad_ref, delta_out, first_buf, second_buf, grad_buf, sem):
    experts = delta_out.shape[0]

    def copies(expert, entry):
        block = list_ref[expert * MAXCH + entry]
        rows = pl.ds(pl.multiple_of(block * BLOCK_ROWS, BLOCK_ROWS), BLOCK_ROWS)
        pair = pl.ds(pl.multiple_of(block // 2 * (2 * BLOCK_ROWS), 2 * BLOCK_ROWS), 2 * BLOCK_ROWS)
        return (
            pltpu.make_async_copy(first_ref.at[expert, rows, :], first_buf.at[expert, entry], sem.at[0, expert, entry]),
            pltpu.make_async_copy(second_ref.at[expert, rows, :], second_buf.at[expert, entry], sem.at[1, expert, entry]),
            pltpu.make_async_copy(grad_ref.at[expert, pair, :], grad_buf.at[expert, entry], sem.at[2, expert, entry]),
        )

    for expert in range(experts):
        for entry in range(MAXCH):
            for copy in copies(expert, entry):
                copy.start()
    for expert in range(experts):
        parts = []
        for entry in range(MAXCH):
            for copy in copies(expert, entry):
                copy.wait()
            odd = list_ref[expert * MAXCH + entry] % 2 == 1
            grads = grad_buf[expert, entry].astype(F32)
            grad = jnp.where(odd, grads[BLOCK_ROWS:], grads[:BLOCK_ROWS])
            first = BETA_ONE * first_buf[expert, entry] + (1.0 - BETA_ONE) * grad
            second = BETA_TWO * second_buf[expert, entry] + (1.0 - BETA_TWO) * grad * grad
            step = LEARN_RATE * (first / FIRST_FIX) / (jnp.sqrt(second / SECOND_FIX) + ADAM_EPS)
            parts.append(jnp.where(entry < count_ref[expert], -step, 0.0))
        delta_out[expert] = jnp.concatenate(parts, axis=0).astype(BF16)


def listed_deltas(adam_first, adam_second, gradient, block_list, block_count):
    experts, _, cols = adam_first.shape
    hbm = pl.BlockSpec(memory_space=pltpu.HBM)
    return pl.pallas_call(
        delta_kernel,
        grid_spec=pltpu.PrefetchScalarGridSpec(
            num_scalar_prefetch=2,
            grid=(),
            in_specs=[hbm, hbm, hbm],
            out_specs=pl.BlockSpec(memory_space=pltpu.VMEM),
            scratch_shapes=[
                pltpu.VMEM((experts, MAXCH, BLOCK_ROWS, cols), F32),
                pltpu.VMEM((experts, MAXCH, BLOCK_ROWS, cols), F32),
                pltpu.VMEM((experts, MAXCH, 2 * BLOCK_ROWS, cols), BF16),
                pltpu.SemaphoreType.DMA((3, experts, MAXCH)),
            ],
        ),
        out_shape=jax.ShapeDtypeStruct((experts, MAXCH * BLOCK_ROWS, cols), BF16),
        compiler_params=pltpu.CompilerParams(vmem_limit_bytes=SMALL_VMEM),
        cost_estimate=pl.CostEstimate(flops=10**6, bytes_accessed=experts * MAXCH * 96 * cols, transcendentals=0),
        name="listed_deltas",
    )(block_list, block_count, in_hbm(adam_first), in_hbm(adam_second), in_hbm(gradient))


def adam_kernel(first_ref, second_ref, grad_ref, *refs):
    first_out, second_out = refs[-2:]
    grad = grad_ref[...].astype(F32)
    first_out[...] = BETA_ONE * first_ref[...] + (1.0 - BETA_ONE) * grad
    second_out[...] = BETA_TWO * second_ref[...] + (1.0 - BETA_TWO) * grad * grad


def adam_part(adam_first, adam_second, gradient, begin, end, filled=()):
    _, rows, cols = adam_first.shape
    block = pl.BlockSpec((1, rows, cols), lambda e: (begin + e, 0, 0))
    size = (end - begin) * rows * cols
    return pl.pallas_call(
        adam_kernel,
        grid=(end - begin,),
        in_specs=[block, block, block] + [pl.BlockSpec(memory_space=pltpu.HBM)] * len(filled),
        out_specs=[block, block],
        out_shape=[jax.ShapeDtypeStruct(adam_first.shape, F32)] * 2,
        input_output_aliases={3 + i: i for i in range(len(filled))},
        compiler_params=pltpu.CompilerParams(vmem_limit_bytes=SMALL_VMEM),
        cost_estimate=pl.CostEstimate(flops=8 * size, bytes_accessed=18 * size, transcendentals=0),
        name="adam_moments",
    )(in_hbm(adam_first), in_hbm(adam_second), in_hbm(gradient), *filled)


def gate_up_kernel(begin, shares, across, within, first, last, meta_ref, own_ref, *refs):
    recv = [refs[i * within : (i + 1) * within] for i in range(shares)]
    refs = refs[shares * within :]
    if first:
        gate_up_ref, out_ref, rows_ref = refs
    else:
        gate_up_ref, sums_ref, out_ref, rows_ref = refs
    expert, share = pl.program_id(0), pl.program_id(2)
    owned, slots = rows_ref.shape[1:3]
    tile = gate_up_ref.shape[3]
    cols = recv[0][0].shape[2]
    per_expert = own_ref.shape[0] // owned
    groups = slots // per_expert

    @pl.when((expert == 0) & (pl.program_id(1) == 0) & (share == 0))
    def _():
        for i in range(shares):
            for q in range(within):
                place = meta_ref[1 + across + q]
                start = (meta_ref[1 + begin + i] * within + place) * cols
                lanes = pl.ds(pl.multiple_of(start, cols), cols)
                into = pl.ds(pl.multiple_of(place * cols, cols), cols)
                for e in range(owned):
                    mine = slice(e * per_expert, (e + 1) * per_expert)
                    rows_ref[i, e, 0:per_expert, into] = own_ref[mine, lanes]
                    for k in range(1, groups):
                        rows_ref[i, e, k * per_expert : (k + 1) * per_expert, into] = recv[i][q][k - 1, mine, :]

    rows = rows_ref[share, expert]
    units = pl.ds(pl.multiple_of(pl.program_id(1) * tile, tile), tile)
    gate = jnp.dot(rows, gate_up_ref[0, 0], preferred_element_type=F32)
    up = jnp.dot(rows, gate_up_ref[0, 1], preferred_element_type=F32)
    if last:
        gate, up = gate + sums_ref[expert, 0, :, units], up + sums_ref[expert, 1, :, units]
        out_ref[expert, :, units] = (gate * jax.nn.sigmoid(gate) * up).astype(BF16)
    elif first:
        out_ref[expert, 0, :, units] = gate
        out_ref[expert, 1, :, units] = up
    else:

        @pl.when(share == 0)
        def _():
            out_ref[expert, 0, :, units] = sums_ref[expert, 0, :, units] + gate
            out_ref[expert, 1, :, units] = sums_ref[expert, 1, :, units] + up

        @pl.when(share > 0)
        def _():
            out_ref[expert, 0, :, units] += gate
            out_ref[expert, 1, :, units] += up


def gate_up_stage(meta, begin, across, own, received, gate_up, sums, last):
    owned, _, width, units = gate_up.shape
    shares, within = len(received), len(received[0])
    assert shares == 1 or not (last or sums is None)
    depth = within * received[0][0].shape[2]
    slots = own.shape[0] // owned * (1 + received[0][0].shape[0])
    tile = min(UNIT_TILE, units)
    vmem = pl.BlockSpec(memory_space=pltpu.VMEM)
    first = sums is None
    if last:
        out_shape = jax.ShapeDtypeStruct((owned, slots, units), BF16)
    else:
        out_shape = jax.ShapeDtypeStruct((owned, 2, slots, units), F32)
    inputs = [own, *sum([list(r) for r in received], []), in_hbm(gate_up)]
    return pl.pallas_call(
        functools.partial(gate_up_kernel, begin, shares, across, within, first, last),
        grid_spec=pltpu.PrefetchScalarGridSpec(
            num_scalar_prefetch=1,
            grid=(owned, units // tile, shares),
            in_specs=[vmem] * (1 + shares * within)
            + [pl.BlockSpec((1, 2, depth, tile), lambda e, j, i, meta: (e, 0, meta[1 + begin + i], j))]
            + ([] if first else [vmem]),
            out_specs=vmem,
            scratch_shapes=[pltpu.VMEM((shares, owned, slots, depth), BF16)],
        ),
        out_shape=out_shape,
        input_output_aliases={} if first or last else {1 + len(inputs): 0},
        compiler_params=pltpu.CompilerParams(vmem_limit_bytes=STAGE_VMEM),
        cost_estimate=pl.CostEstimate(
            flops=4 * owned * slots * depth * units * shares,
            bytes_accessed=4 * owned * depth * units * shares,
            transcendentals=0,
        ),
        name="gate_up_stage",
    )(meta, *inputs, *([] if first else [sums]))


def fetch_kernel(down_ref, out_ref, sem):
    copies = [
        pltpu.make_async_copy(down_ref.at[e], out_ref.at[e], sem.at[e]) for e in range(down_ref.shape[0])
    ]
    for copy in copies:
        copy.start()
    for copy in copies:
        copy.wait()


def fetch_down(down_weight):
    return pl.pallas_call(
        fetch_kernel,
        in_specs=[pl.BlockSpec(memory_space=pltpu.HBM)],
        out_specs=pl.BlockSpec(memory_space=pltpu.VMEM),
        out_shape=pltpu.VMEM(down_weight.shape, down_weight.dtype),
        scratch_shapes=[pltpu.SemaphoreType.DMA((down_weight.shape[0],))],
        compiler_params=pltpu.CompilerParams(vmem_limit_bytes=SMALL_VMEM),
        cost_estimate=pl.CostEstimate(flops=0, bytes_accessed=2 * down_weight.size, transcendentals=0),
        name="fetch_down",
    )(in_hbm(down_weight))


def down_kernel(share, across, within, per_expert, meta_ref, list_ref, hidden_ref, delta_ref, down_ref, *outs):
    owned, units, _ = down_ref.shape
    cols = outs[0].shape[1]
    src_cols = delta_ref.shape[3]
    groups = hidden_ref.shape[1] // per_expert
    listed = MAXCH * BLOCK_ROWS
    span = BLOCK_ROWS * STRIDE
    row = lax.broadcasted_iota(jnp.int32, (MAXCH * span, listed), 0)
    col = lax.broadcasted_iota(jnp.int32, (MAXCH * span, listed), 1)
    spread = ((row // STRIDE == col) & (row % STRIDE == 0)).astype(F32).astype(BF16)
    unit = lax.broadcasted_iota(jnp.int32, (1, units), 1)
    line = lax.broadcasted_iota(jnp.int32, (units, MAXCH * span), 0)
    place = lax.broadcasted_iota(jnp.int32, (units, MAXCH * span), 1)
    blocks, rest, taken = [], [], []
    for e in range(owned):
        blocks.append([list_ref[(meta_ref[0] * owned + e) * MAXCH + entry] for entry in range(MAXCH)])
        hit = unit // span == blocks[e][0]
        base = jnp.zeros_like(place)
        for entry in range(MAXCH):
            hit = hit | (unit // span == blocks[e][entry])
            base = jnp.where(place // span == entry, blocks[e][entry] * span, base)
        pick = jnp.where(line == base + place % span, 1.0, 0.0).astype(BF16)
        taken.append(jnp.dot(hidden_ref[e], pick, preferred_element_type=F32).astype(BF16))
        rest.append(hidden_ref[e] * jnp.where(hit, 0.0, 1.0).astype(BF16))
    for q in list(range(1, within)) + [0]:
        first_col = (meta_ref[1 + share] * within + meta_ref[1 + across + q]) * cols
        source = first_col // src_cols
        there = pl.ds(pl.multiple_of(first_col - source * src_cols, cols), cols)
        lanes = pl.ds(pl.multiple_of(first_col, cols), cols)
        for e in range(owned):
            added = jnp.dot(spread, delta_ref[source, e, :, there], preferred_element_type=F32)
            old = jnp.concatenate(
                [down_ref[e, pl.ds(pl.multiple_of(b * span, span), span), lanes] for b in blocks[e]], axis=0
            )
            fresh = (old.astype(F32) + added).astype(BF16)
            part = jnp.dot(rest[e], down_ref[e, :, lanes], preferred_element_type=F32)
            part = (part + jnp.dot(taken[e], fresh, preferred_element_type=F32)).astype(BF16)
            for k in range(groups):
                at = (k * owned + e) * per_expert
                outs[q][at : at + per_expert, :] = part[k * per_expert : (k + 1) * per_expert]


def down_pieces(meta, share, across, within, per_expert, block_list, hidden, delta, down_weight, cols):
    owned, units, _ = down_weight.shape
    slots = hidden.shape[1]
    rows = owned * slots
    vmem = pl.BlockSpec(memory_space=pltpu.VMEM)
    return pl.pallas_call(
        functools.partial(down_kernel, share, across, within, per_expert),
        grid_spec=pltpu.PrefetchScalarGridSpec(
            num_scalar_prefetch=2, grid=(), in_specs=[vmem] * 3, out_specs=[vmem] * within
        ),
        out_shape=[jax.ShapeDtypeStruct((rows, cols), BF16)] * within,
        compiler_params=pltpu.CompilerParams(vmem_limit_bytes=SMALL_VMEM),
        cost_estimate=pl.CostEstimate(
            flops=2 * owned * slots * units * cols * within,
            bytes_accessed=2 * owned * units * cols * within,
            transcendentals=0,
        ),
        name="down_mixed",
    )(meta, block_list, hidden, delta, down_weight)


def swap(value, axis, distance):
    return lax.ppermute(value, axis, [(i, i ^ distance) for i in range(lax.axis_size(axis))])


def shift(value, axis, distance):
    size = lax.axis_size(axis)
    return lax.ppermute(value, axis, [(i, (i + distance) % size) for i in range(size)])


def on_device(
    tokens,
    route,
    route_weight,
    gate_up,
    down_weight,
    adam_first,
    adam_second,
    gradient,
    block_list,
    block_count,
):
    groups = lax.axis_size("expert")
    across, within = lax.axis_size("fsdp"), lax.axis_size("tensor")
    at_z, at_f, at_t = lax.axis_index("expert"), lax.axis_index("fsdp"), lax.axis_index("tensor")
    owned = gate_up.shape[0]
    steps, block, width = tokens.shape
    cols = width // (across * within)
    lists = block_list.reshape(-1)
    counts = block_count.reshape(-1)

    meta = jnp.stack(
        [at_z]
        + [at_f ^ r for r in range(across)]
        + [at_t ^ q for q in range(within)]
        + [at_f * within + at_t]
    ).astype(jnp.int32)

    *sends, mine, pick = pack_slots(meta, tokens, route, groups, owned, cols)
    arrived = [shift(send, "expert", k) for k, send in enumerate(sends, 1)]
    delta = listed_deltas(adam_first, adam_second, gradient, lists, counts)
    down_local = fetch_down(down_weight)
    arrived, delta, down_local = lax.optimization_barrier((arrived, delta, down_local))
    away = jnp.stack(arrived)
    by_owner = delta.reshape(groups, owned, *delta.shape[1:])
    incoming = lax.all_to_all(by_owner, "expert", split_axis=0, concat_axis=0, tiled=True)

    def stage(begin, columns, sums, last):
        received = [[c] + [swap(c, "tensor", q) for q in range(1, within)] for c in columns]
        return gate_up_stage(meta, begin, across, mine, received, gate_up, sums, last)

    near = [swap(away, "fsdp", r) for r in range(1, across - 1)]
    sums = stage(0, [away], None, False)
    away, sums = lax.optimization_barrier((away, sums))
    far = swap(away, "fsdp", across - 1)
    near, sums = lax.optimization_barrier((near, sums))
    sums = stage(1, near, sums, False)
    incoming, far, sums = lax.optimization_barrier((incoming, far, sums))
    hidden = stage(across - 1, [far], sums, True)

    def down(r, order):
        pieces = down_pieces(order, r, across, within, steps * CAP, lists, hidden, incoming, down_local, cols)
        return pieces[0], [swap(pieces[q], "tensor", q) for q in range(1, within)]

    def add(*terms):
        total = terms[0].astype(F32)
        for term in terms[1:]:
            total = total + term.astype(F32)
        return total.astype(BF16)

    rows = groups * owned * steps * CAP
    upper, lower = slice(0, rows // 2), slice(rows // 2, rows)

    def summed(pair, at):
        return add(pair[0][at], *[other[at] for other in pair[1]])

    if across == 4:
        far = down(3, meta)
        one = down(1, meta)
        far_up, far_low = summed(far, upper), summed(far, lower)
        order, far_up, far_low = lax.optimization_barrier((meta, far_up, far_low))
        by_one, by_two = swap(far_up, "fsdp", 1), swap(far_low, "fsdp", 2)
        two = down(2, order)
        one_sum = add(one[0], *one[1], jnp.pad(by_two, ((rows // 2, 0), (0, 0))))
        order, one_sum = lax.optimization_barrier((order, one_sum))
        others = [swap(one_sum, "fsdp", 1)]
        own = down(0, order)
        two_sum = add(two[0], *two[1], jnp.pad(by_one, ((0, rows // 2), (0, 0))))
        others.append(swap(two_sum, "fsdp", 2))
    else:
        others = [swap(summed(down(r, meta), slice(0, rows)), "fsdp", r) for r in range(1, across)]
        own = down(0, meta)
    middle = adam_first.shape[0] // 2
    adam_in, own = lax.optimization_barrier(((adam_first, adam_second, gradient), own))
    filled = adam_part(*adam_in, 0, middle)
    parts = add(own[0], *own[1], *others).reshape(groups, rows // groups, cols)
    adam_in, filled, parts = lax.optimization_barrier((adam_in, filled, parts))
    back = [shift(parts[k], "expert", -k) for k in range(1, groups)]
    first_new, second_new = adam_part(*adam_in, middle, adam_first.shape[0], filled)
    return (combine_slots(pick, route_weight, [parts[0], *back]), first_new, second_new)


def solution(mesh):
    return jax.shard_map(
        on_device,
        mesh=mesh,
        in_specs=(
            P(None, "expert", None),
            P(None, "expert", None),
            P(None, "expert", None),
            P("expert", None, None, ("fsdp", "tensor")),
            P("expert", ("fsdp", "tensor"), None),
            P(None, ("fsdp", "tensor"), "expert"),
            P(None, ("fsdp", "tensor"), "expert"),
            P(None, ("fsdp", "tensor"), "expert"),
            P(None, ("fsdp", "tensor"), None),
            P(None, ("fsdp", "tensor")),
        ),
        out_specs=(
            P(None, "expert", ("fsdp", "tensor")),
            P(None, ("fsdp", "tensor"), "expert"),
            P(None, ("fsdp", "tensor"), "expert"),
        ),
        check_vma=False,
    )
```

```python
import functools

import jax
import jax.numpy as jnp
from jax import lax
from jax.experimental import pallas as pl
from jax.experimental.pallas import tpu as pltpu
from jax.sharding import PartitionSpec as P

STRIDE = 4
BLOCK_ROWS = 8
MAXCH = 4
CAP = 32
PIECES = 2
UNIT_TILE = 256

BETA_ONE = 0.9
BETA_TWO = 0.95
LEARN_RATE = 0.03
ADAM_EPS = 1e-08
FIRST_FIX = 1.0 - 0.9**10
SECOND_FIX = 1.0 - 0.95**10

SHORT = pl.CostEstimate(flops=1, bytes_accessed=1, transcendentals=0)

F32 = jnp.float32
BF16 = jnp.bfloat16
SMALL_VMEM = 16 * 2**20
STAGE_VMEM = 20 * 2**20


def in_hbm(value):
    return pltpu.with_memory_space_constraint(value, pltpu.HBM)


def as_column(ref, k):
    row = jnp.concatenate([ref[s, k : k + 1, :].astype(F32) for s in range(ref.shape[0])], axis=1)
    return jnp.transpose(jnp.broadcast_to(row, (row.shape[1], row.shape[1])))[:, 0:1]


def pack_kernel(groups, owned, block, meta_ref, tokens_ref, route_ref, *refs):
    sends, (select_ref, pick_ref, share, sem) = refs[: groups - 1], refs[groups - 1 :]
    rows, cols = share.shape
    steps = rows // block
    lanes = pl.ds(pl.multiple_of(meta_ref[meta_ref.shape[0] - 1] * cols, cols), cols)
    copies = [
        pltpu.make_async_copy(tokens_ref.at[s, :, lanes], share.at[pl.ds(s * block, block)], sem.at[s])
        for s in range(steps)
    ]
    for copy in copies:
        copy.start()
    per_expert = steps * CAP
    per_group = owned * per_expert
    slots = groups * per_group
    token = lax.broadcasted_iota(jnp.int32, (rows, rows), 0)
    lane = lax.broadcasted_iota(jnp.int32, (rows, rows), 1)
    before = jnp.where((lane < token) & (lane // block == token // block), 1.0, 0.0).astype(BF16)
    named = [as_column(route_ref, k) for k in range(2)]
    lane = lane.astype(F32)
    member = jnp.where((lane == named[0]) | (lane == named[1]), 1.0, 0.0).astype(BF16)
    earlier = jnp.dot(before, member, preferred_element_type=F32)
    slot = lax.broadcasted_iota(jnp.int32, (rows, slots), 1)
    step = lax.broadcasted_iota(jnp.int32, (rows, slots), 0) // block
    group = (meta_ref[0] + slot // per_group) % groups
    expert = (group * owned + slot % per_group // per_expert).astype(F32)
    here = slot % per_expert // CAP == step
    spot = (slot % CAP).astype(F32)
    total = jnp.zeros((rows, slots), F32)
    for k in range(2):
        position = jnp.sum(jnp.where(lane == named[k], earlier, 0.0), axis=1, keepdims=True)
        pick = jnp.where((expert == named[k]) & here & (spot == position), 1.0, 0.0)
        pick_ref[k] = pick.astype(BF16)
        total = total + pick
    select = jnp.transpose(total).astype(BF16)
    select_ref[...] = select[:per_group]
    for copy in copies:
        copy.wait()
    for k in range(1, groups):
        sends[k - 1][...] = jnp.dot(
            select[k * per_group : (k + 1) * per_group], share[...], preferred_element_type=F32
        ).astype(BF16)


def pack_slots(meta, tokens, route, groups, owned, cols):
    steps, block, width = tokens.shape
    rows = steps * block
    per_group = owned * steps * CAP
    vmem = pl.BlockSpec(memory_space=pltpu.VMEM)
    return pl.pallas_call(
        functools.partial(pack_kernel, groups, owned, block),
        grid_spec=pltpu.PrefetchScalarGridSpec(
            num_scalar_prefetch=1,
            grid=(),
            in_specs=[pl.BlockSpec(memory_space=pltpu.HBM), vmem],
            out_specs=[vmem] * (groups + 1),
            scratch_shapes=[pltpu.VMEM((rows, cols), BF16), pltpu.SemaphoreType.DMA((steps,))],
        ),
        out_shape=[jax.ShapeDtypeStruct((per_group, cols), BF16)] * (groups - 1)
        + [
            jax.ShapeDtypeStruct((per_group, rows), BF16),
            jax.ShapeDtypeStruct((2, rows, groups * per_group), BF16),
        ],
        compiler_params=pltpu.CompilerParams(vmem_limit_bytes=SMALL_VMEM),
        cost_estimate=pl.CostEstimate(flops=10**7, bytes_accessed=4 * rows * cols, transcendentals=0),
        name="pack_slots",
    )(meta, in_hbm(tokens), route.transpose(0, 2, 1))


def own_kernel(select_ref, tokens_ref, out_ref):
    every = jnp.concatenate([tokens_ref[s] for s in range(tokens_ref.shape[0])], axis=0)
    out_ref[...] = jnp.dot(select_ref[...], every, preferred_element_type=F32).astype(BF16)


def own_slots(select, tokens):
    vmem = pl.BlockSpec(memory_space=pltpu.VMEM)
    return pl.pallas_call(
        own_kernel,
        in_specs=[vmem, vmem],
        out_specs=vmem,
        out_shape=jax.ShapeDtypeStruct((select.shape[0], tokens.shape[2]), BF16),
        compiler_params=pltpu.CompilerParams(vmem_limit_bytes=SMALL_VMEM),
        cost_estimate=pl.CostEstimate(flops=10**8, bytes_accessed=4 * tokens.size, transcendentals=0),
        name="own_slots",
    )(select, tokens)


def combine_kernel(pick_ref, weight_ref, *refs):
    out_ref = refs[-1]
    steps, block, _ = out_ref.shape
    rows = jnp.concatenate([ref[...] for ref in refs[:-1]], axis=0)
    total = jnp.zeros((steps * block, out_ref.shape[2]), F32)
    for k in range(2):
        total = total + as_column(weight_ref, k) * jnp.dot(pick_ref[k], rows, preferred_element_type=F32)
    for s in range(steps):
        out_ref[s] = total[s * block : (s + 1) * block].astype(BF16)


def combine_slots(pick, weight, parts):
    steps, block, _ = weight.shape
    cols = parts[0].shape[1]
    vmem = pl.BlockSpec(memory_space=pltpu.VMEM)
    return pl.pallas_call(
        combine_kernel,
        in_specs=[vmem] * (2 + len(parts)),
        out_specs=vmem,
        out_shape=jax.ShapeDtypeStruct((steps, block, cols), BF16),
        compiler_params=pltpu.CompilerParams(vmem_limit_bytes=SMALL_VMEM),
        cost_estimate=pl.CostEstimate(flops=10**7, bytes_accessed=10**6, transcendentals=0),
        name="combine_slots",
    )(pick, weight.transpose(0, 2, 1), *parts)


def delta_kernel(groups, meta_ref, list_ref, count_ref, first_ref, second_ref, grad_ref, *refs):
    outs, (first_buf, second_buf, grad_buf, sem) = refs[:groups], refs[groups:]
    owned = outs[0].shape[0]

    def copies(at, entry):
        expert = lax.rem(meta_ref[0] + at // owned, groups) * owned + at % owned
        block = list_ref[expert, entry]
        rows = pl.ds(pl.multiple_of(block * BLOCK_ROWS, BLOCK_ROWS), BLOCK_ROWS)
        pair = pl.ds(pl.multiple_of(block // 2 * (2 * BLOCK_ROWS), 2 * BLOCK_ROWS), 2 * BLOCK_ROWS)
        return (
            pltpu.make_async_copy(first_ref.at[expert, rows, :], first_buf.at[at, entry], sem.at[0, at, entry]),
            pltpu.make_async_copy(second_ref.at[expert, rows, :], second_buf.at[at, entry], sem.at[1, at, entry]),
            pltpu.make_async_copy(grad_ref.at[expert, pair, :], grad_buf.at[at, entry], sem.at[2, at, entry]),
        )

    order = [(k % groups) * owned + e for k in range(1, groups + 1) for e in range(owned)]
    for at in order:
        for entry in range(MAXCH):
            for copy in copies(at, entry):
                copy.start()
    for at in order:
        expert = lax.rem(meta_ref[0] + at // owned, groups) * owned + at % owned
        parts = []
        for entry in range(MAXCH):
            for copy in copies(at, entry):
                copy.wait()
            odd = list_ref[expert, entry] % 2 == 1
            grads = grad_buf[at, entry].astype(F32)
            grad = jnp.where(odd, grads[BLOCK_ROWS:], grads[:BLOCK_ROWS])
            first = BETA_ONE * first_buf[at, entry] + (1.0 - BETA_ONE) * grad
            second = BETA_TWO * second_buf[at, entry] + (1.0 - BETA_TWO) * grad * grad
            step = LEARN_RATE * (first / FIRST_FIX) / (jnp.sqrt(second / SECOND_FIX) + ADAM_EPS)
            parts.append(jnp.where(entry < count_ref[expert], -step, 0.0))
        outs[at // owned][at % owned] = jnp.concatenate(parts, axis=0).astype(BF16)


def listed_deltas(meta, adam_first, adam_second, gradient, block_list, block_count, groups):
    experts, _, cols = adam_first.shape
    hbm = pl.BlockSpec(memory_space=pltpu.HBM)
    return pl.pallas_call(
        functools.partial(delta_kernel, groups),
        grid_spec=pltpu.PrefetchScalarGridSpec(
            num_scalar_prefetch=3,
            grid=(),
            in_specs=[hbm, hbm, hbm],
            out_specs=[pl.BlockSpec(memory_space=pltpu.VMEM)] * groups,
            scratch_shapes=[
                pltpu.VMEM((experts, MAXCH, BLOCK_ROWS, cols), F32),
                pltpu.VMEM((experts, MAXCH, BLOCK_ROWS, cols), F32),
                pltpu.VMEM((experts, MAXCH, 2 * BLOCK_ROWS, cols), BF16),
                pltpu.SemaphoreType.DMA((3, experts, MAXCH)),
            ],
        ),
        out_shape=[jax.ShapeDtypeStruct((experts // groups, MAXCH * BLOCK_ROWS, cols), BF16)] * groups,
        compiler_params=pltpu.CompilerParams(vmem_limit_bytes=SMALL_VMEM),
        cost_estimate=pl.CostEstimate(flops=10**6, bytes_accessed=experts * MAXCH * 96 * cols, transcendentals=0),
        name="listed_deltas",
    )(meta, block_list, block_count, in_hbm(adam_first), in_hbm(adam_second), in_hbm(gradient))


def adam_kernel(first_ref, second_ref, grad_ref, *refs):
    first_out, second_out = refs[-2:]
    grad = grad_ref[...].astype(F32)
    first_out[...] = BETA_ONE * first_ref[...] + (1.0 - BETA_ONE) * grad
    second_out[...] = BETA_TWO * second_ref[...] + (1.0 - BETA_TWO) * grad * grad


def adam_part(adam_first, adam_second, gradient, begin, end, filled=(), cost=None):
    _, rows, cols = adam_first.shape
    block = pl.BlockSpec((1, rows, cols), lambda e: (begin + e, 0, 0))
    size = (end - begin) * rows * cols
    return pl.pallas_call(
        adam_kernel,
        grid=(end - begin,),
        in_specs=[block, block, block] + [pl.BlockSpec(memory_space=pltpu.HBM)] * len(filled),
        out_specs=[block, block],
        out_shape=[jax.ShapeDtypeStruct(adam_first.shape, F32)] * 2,
        input_output_aliases={3 + i: i for i in range(len(filled))},
        compiler_params=pltpu.CompilerParams(vmem_limit_bytes=SMALL_VMEM),
        cost_estimate=cost or pl.CostEstimate(flops=8 * size, bytes_accessed=18 * size, transcendentals=0),
        name="adam_moments",
    )(in_hbm(adam_first), in_hbm(adam_second), in_hbm(gradient), *filled)


def gate_up_kernel(begin, shares, across, within, first, last, meta_ref, list_ref, own_ref, *refs):
    recv = [refs[i * within : (i + 1) * within] for i in range(shares)]
    refs = refs[shares * within :]
    weights, refs = refs[:shares], refs[shares:]
    sums_ref, refs = (None, refs) if first else (refs[0], refs[1:])
    out_ref, taken_ref, rows_ref = (refs[0], None, refs[1]) if not last else refs
    expert = pl.program_id(0)
    owned, slots = rows_ref.shape[1:3]
    tile = weights[0].shape[3]
    cols = recv[0][0].shape[2]
    per_expert = own_ref.shape[0] // owned
    groups = slots // per_expert

    @pl.when((expert == 0) & (pl.program_id(1) == 0))
    def _():
        for i in range(shares):
            for q in range(within):
                place = meta_ref[1 + across + q]
                start = (meta_ref[1 + begin + i] * within + place) * cols
                lanes = pl.ds(pl.multiple_of(start, cols), cols)
                into = pl.ds(pl.multiple_of(place * cols, cols), cols)
                for e in range(owned):
                    mine = slice(e * per_expert, (e + 1) * per_expert)
                    rows_ref[i, e, 0:per_expert, into] = own_ref[mine, lanes]
                    for k in range(1, groups):
                        rows_ref[i, e, k * per_expert : (k + 1) * per_expert, into] = recv[i][q][k - 1, mine, :]

    first_unit = pl.program_id(1) * tile
    units = pl.ds(pl.multiple_of(first_unit, tile), tile)

    def product(side):
        total = jnp.dot(rows_ref[0, expert], weights[0][0, side], preferred_element_type=F32)
        for i in range(1, shares):
            total = total + jnp.dot(rows_ref[i, expert], weights[i][0, side], preferred_element_type=F32)
        return total if first else total + sums_ref[expert, side, :, units]

    if not last:
        for side in range(2):
            out_ref[expert, side, :, units] = product(side)
        return
    gate, up = product(0), product(1)
    hidden = (gate * jax.nn.sigmoid(gate) * up).astype(BF16)
    span = BLOCK_ROWS * STRIDE
    unit = first_unit + lax.broadcasted_iota(jnp.int32, (1, tile), 1)
    line = first_unit + lax.broadcasted_iota(jnp.int32, (tile, MAXCH * span), 0)
    place = lax.broadcasted_iota(jnp.int32, (tile, MAXCH * span), 1)
    hit = unit < 0
    source = place % span
    for entry in range(MAXCH):
        block = list_ref[meta_ref[0] * owned + expert, entry]
        hit = hit | (unit // span == block)
        source = source + jnp.where(place // span == entry, block * span, 0)
    pick = jnp.where(line == source, 1.0, 0.0).astype(BF16)
    taken = jnp.dot(hidden, pick, preferred_element_type=F32).astype(BF16)
    out_ref[expert, :, units] = hidden * jnp.where(hit, 0.0, 1.0).astype(BF16)

    @pl.when(pl.program_id(1) == 0)
    def _():
        taken_ref[expert] = taken

    @pl.when(pl.program_id(1) > 0)
    def _():
        taken_ref[expert] += taken


def gate_up_stage(meta, block_list, begin, across, own, received, gate_up, sums, last):
    owned, _, width, units = gate_up.shape
    shares, within = len(received), len(received[0])
    depth = within * received[0][0].shape[2]
    slots = own.shape[0] // owned * (1 + received[0][0].shape[0])
    tile = min(UNIT_TILE, units)
    vmem = pl.BlockSpec(memory_space=pltpu.VMEM)
    first = sums is None
    if last:
        out_shape = [
            jax.ShapeDtypeStruct((owned, slots, units), BF16),
            jax.ShapeDtypeStruct((owned, slots, MAXCH * BLOCK_ROWS * STRIDE), BF16),
        ]
    else:
        out_shape = [jax.ShapeDtypeStruct((owned, 2, slots, units), F32)]
    weights = [
        pl.BlockSpec((1, 2, depth, tile), lambda e, j, meta, _, i=i: (e, 0, meta[1 + begin + i], j))
        for i in range(shares)
    ]
    inputs = [own, *sum([list(r) for r in received], []), *[in_hbm(gate_up)] * shares]
    return pl.pallas_call(
        functools.partial(gate_up_kernel, begin, shares, across, within, first, last),
        grid_spec=pltpu.PrefetchScalarGridSpec(
            num_scalar_prefetch=2,
            grid=(owned, units // tile),
            in_specs=[vmem] * (1 + shares * within) + weights + ([] if first else [vmem]),
            out_specs=[vmem] * len(out_shape),
            scratch_shapes=[pltpu.VMEM((shares, owned, slots, depth), BF16)],
        ),
        out_shape=out_shape,
        input_output_aliases={} if first or last else {2 + len(inputs): 0},
        compiler_params=pltpu.CompilerParams(vmem_limit_bytes=STAGE_VMEM),
        cost_estimate=pl.CostEstimate(
            flops=4 * owned * slots * depth * units * shares,
            bytes_accessed=4 * owned * depth * units * shares,
            transcendentals=0,
        ),
        name="gate_up_stage",
    )(meta, block_list, *inputs, *([] if first else [sums]))


def fetch_kernel(down_ref, out_ref, sem):
    copies = [
        pltpu.make_async_copy(down_ref.at[e], out_ref.at[e], sem.at[e]) for e in range(down_ref.shape[0])
    ]
    for copy in copies:
        copy.start()
    for copy in copies:
        copy.wait()


def fetch_down(down_weight):
    return pl.pallas_call(
        fetch_kernel,
        in_specs=[pl.BlockSpec(memory_space=pltpu.HBM)],
        out_specs=pl.BlockSpec(memory_space=pltpu.VMEM),
        out_shape=pltpu.VMEM(down_weight.shape, down_weight.dtype),
        scratch_shapes=[pltpu.SemaphoreType.DMA((down_weight.shape[0],))],
        compiler_params=pltpu.CompilerParams(vmem_limit_bytes=SMALL_VMEM),
        cost_estimate=pl.CostEstimate(flops=0, bytes_accessed=2 * down_weight.size, transcendentals=0),
        name="fetch_down",
    )(in_hbm(down_weight))


def down_kernel(share, across, within, per_expert, meta_ref, list_ref, rest_ref, taken_ref, delta_ref, down_ref, *outs):
    owned = down_ref.shape[0]
    rows, cols = outs[0].shape
    src_cols = delta_ref.shape[3]
    groups = rest_ref.shape[1] // per_expert
    listed = MAXCH * BLOCK_ROWS
    span = BLOCK_ROWS * STRIDE
    row = lax.broadcasted_iota(jnp.int32, (MAXCH * span, listed), 0)
    col = lax.broadcasted_iota(jnp.int32, (MAXCH * span, listed), 1)
    spread = ((row // STRIDE == col) & (row % STRIDE == 0)).astype(F32).astype(BF16)
    for q in list(range(1, within)) + [0]:
        first_col = (meta_ref[1 + share] * within + meta_ref[1 + across + q]) * cols
        source = first_col // src_cols
        there = pl.ds(pl.multiple_of(first_col - source * src_cols, cols), cols)
        lanes = pl.ds(pl.multiple_of(first_col, cols), cols)
        distance = lax.rem(meta_ref[0] - source + groups, groups)
        for e in range(owned):
            added = jnp.dot(spread, delta_ref[distance, e, :, there], preferred_element_type=F32)
            old = []
            for entry in range(MAXCH):
                block = list_ref[meta_ref[0] * owned + e, entry]
                old.append(down_ref[e, pl.ds(pl.multiple_of(block * span, span), span), lanes])
            fresh = (jnp.concatenate(old, axis=0).astype(F32) + added).astype(BF16)
            part = jnp.dot(rest_ref[e], down_ref[e, :, lanes], preferred_element_type=F32)
            part = (part + jnp.dot(taken_ref[e], fresh, preferred_element_type=F32)).astype(BF16)
            for k in range(groups):
                at = (k * owned + e) * per_expert
                part_of = PIECES * at // rows
                into = outs[0] if q == 0 else outs[PIECES * (q - 1) + 1 + part_of]
                at = at if q == 0 else at - part_of * (rows // PIECES)
                into[at : at + per_expert, :] = part[k * per_expert : (k + 1) * per_expert]


def down_pieces(meta, share, across, within, per_expert, block_list, rest, taken, delta, down_weight, cols):
    owned, units, _ = down_weight.shape
    slots = rest.shape[1]
    rows = owned * slots
    vmem = pl.BlockSpec(memory_space=pltpu.VMEM)
    return pl.pallas_call(
        functools.partial(down_kernel, share, across, within, per_expert),
        grid_spec=pltpu.PrefetchScalarGridSpec(
            num_scalar_prefetch=2, grid=(), in_specs=[vmem] * 4, out_specs=[vmem] * (1 + PIECES * (within - 1))
        ),
        out_shape=[jax.ShapeDtypeStruct((rows, cols), BF16)]
        + [jax.ShapeDtypeStruct((rows // PIECES, cols), BF16)] * (PIECES * (within - 1)),
        compiler_params=pltpu.CompilerParams(vmem_limit_bytes=SMALL_VMEM),
        cost_estimate=pl.CostEstimate(
            flops=2 * owned * slots * units * cols * within,
            bytes_accessed=2 * owned * units * cols * within,
            transcendentals=0,
        ),
        name="down_mixed",
    )(meta, block_list, rest, taken, delta, down_weight)


def swap(value, axis, distance):
    return lax.ppermute(value, axis, [(i, i ^ distance) for i in range(lax.axis_size(axis))])


def shift(value, axis, distance):
    size = lax.axis_size(axis)
    return lax.ppermute(value, axis, [(i, (i + distance) % size) for i in range(size)])


def on_device(
    tokens,
    route,
    route_weight,
    gate_up,
    down_weight,
    adam_first,
    adam_second,
    gradient,
    block_list,
    block_count,
):
    groups = lax.axis_size("expert")
    across, within = lax.axis_size("fsdp"), lax.axis_size("tensor")
    at_z, at_f, at_t = lax.axis_index("expert"), lax.axis_index("fsdp"), lax.axis_index("tensor")
    owned = gate_up.shape[0]
    steps, block, width = tokens.shape
    cols = width // (across * within)
    lists = block_list.reshape(block_list.shape[0], MAXCH)
    counts = block_count.reshape(-1)

    meta = jnp.stack(
        [at_z]
        + [at_f ^ r for r in range(across)]
        + [at_t ^ q for q in range(within)]
        + [at_f * within + at_t]
    ).astype(jnp.int32)

    *sends, select, pick = pack_slots(meta, tokens, route, groups, owned, cols)
    arrived = [shift(send, "expert", k) for k, send in enumerate(sends, 1)]
    mine = own_slots(select, tokens)
    deltas = listed_deltas(meta, adam_first, adam_second, gradient, lists, counts, groups)
    down_source, deltas = lax.optimization_barrier((down_weight, deltas))
    down_local = fetch_down(down_source)
    arrived, deltas, mine, down_local = lax.optimization_barrier((arrived, deltas, mine, down_local))
    away = jnp.stack(arrived)
    early = {k: shift(deltas[k], "expert", k) for k in (1, groups - 1)}

    def stage(begin, columns, sums, last):
        received = [[c] + [swap(c, "tensor", q) for q in range(1, within)] for c in columns]
        return gate_up_stage(meta, lists, begin, across, mine, received, gate_up, sums, last)

    others = [swap(away, "fsdp", r) for r in range(1, across)]
    (sums,) = stage(0, [away], None, False)
    experts = adam_first.shape[0]
    parts_at = (experts // 4, experts // 4 + experts * 3 // 8, experts)
    adam_in = (adam_first, adam_second, gradient)
    adam_in, deltas, early, sums = lax.optimization_barrier((adam_in, deltas, early, sums))
    late = {k: shift(deltas[k], "expert", k) for k in range(2, groups - 1)}
    filled = adam_part(*adam_in, 0, parts_at[0], cost=SHORT)
    others, late, filled, sums = lax.optimization_barrier((others, late, filled, sums))
    incoming = [{0: deltas[0], **early, **late}[k] for k in range(groups)]
    incoming = jnp.stack(incoming)
    rest, taken = stage(1, others, sums, True)

    def down(r, order):
        pieces = down_pieces(
            order, r, across, within, steps * CAP, lists, rest, taken, incoming, down_local, cols
        )
        return pieces[0], [swap(pieces[i], "tensor", (i - 1) // PIECES + 1) for i in range(1, len(pieces))]

    def add(*terms):
        total = terms[0].astype(F32)
        for term in terms[1:]:
            total = total + term.astype(F32)
        return total.astype(BF16)

    rows = groups * owned * steps * CAP

    def joined(pair):
        return [jnp.concatenate(pair[1][i : i + PIECES]) for i in range(0, len(pair[1]), PIECES)]

    def summed(pair, *more):
        return add(pair[0], *joined(pair), *more)

    far_sum = summed(down(across - 1, meta))
    if across == 4:
        far_up, far_low = far_sum[: rows // 2], far_sum[rows // 2 :]
        order, far_up, far_low = lax.optimization_barrier((meta, far_up, far_low))
        by_one, by_two = swap(far_up, "fsdp", 1), swap(far_low, "fsdp", 2)
        near = [down(r, order) for r in (1, 2)]
        by_one, by_two, near = lax.optimization_barrier((by_one, by_two, near))
        passed = [jnp.pad(by_two, ((rows // 2, 0), (0, 0))), jnp.pad(by_one, ((0, rows // 2), (0, 0)))]
        others = [swap(summed(near[i], passed[i]), "fsdp", i + 1) for i in range(2)]
    else:
        order, far_sum = lax.optimization_barrier((meta, far_sum))
        others = [swap(summed(down(r, order)), "fsdp", r) for r in range(1, across - 1)]
        others.append(swap(far_sum, "fsdp", across - 1))
    last = down(0, order)
    adam_in, filled, raw = lax.optimization_barrier((adam_in, filled, last[0]))
    filled = adam_part(*adam_in, parts_at[0], parts_at[1], filled)
    parts = add(raw, *joined(last), *others).reshape(groups, rows // groups, cols)
    adam_in, filled, parts = lax.optimization_barrier((adam_in, filled, parts))
    back = [shift(parts[k], "expert", -k) for k in range(1, groups)]
    first_new, second_new = adam_part(*adam_in, parts_at[1], parts_at[2], filled)
    return (combine_slots(pick, route_weight, [parts[0], *back]), first_new, second_new)


def solution(mesh):
    return jax.shard_map(
        on_device,
        mesh=mesh,
        in_specs=(
            P(None, "expert", None),
            P(None, "expert", None),
            P(None, "expert", None),
            P("expert", None, None, ("fsdp", "tensor")),
            P("expert", ("fsdp", "tensor"), None),
            P(None, ("fsdp", "tensor"), "expert"),
            P(None, ("fsdp", "tensor"), "expert"),
            P(None, ("fsdp", "tensor"), "expert"),
            P(None, ("fsdp", "tensor"), None),
            P(None, ("fsdp", "tensor")),
        ),
        out_specs=(
            P(None, "expert", ("fsdp", "tensor")),
            P(None, ("fsdp", "tensor"), "expert"),
            P(None, ("fsdp", "tensor"), "expert"),
        ),
        check_vma=False,
    )
```

```python
import functools

import jax
import jax.numpy as jnp
from jax import lax
from jax.experimental import pallas as pl
from jax.experimental.pallas import tpu as pltpu
from jax.sharding import PartitionSpec as P

STRIDE = 4
BLOCK_ROWS = 8
MAXCH = 4
CAP = 32
PIECES = 2
RING = 12
UNIT_TILE = 512

BETA_ONE = 0.9
BETA_TWO = 0.95
LEARN_RATE = 0.03
ADAM_EPS = 1e-08
FIRST_FIX = 1.0 - 0.9**10
SECOND_FIX = 1.0 - 0.95**10

SHORT = pl.CostEstimate(flops=1, bytes_accessed=1, transcendentals=0)

F32 = jnp.float32
BF16 = jnp.bfloat16
SMALL_VMEM = 16 * 2**20
STAGE_VMEM = 24 * 2**20


def in_hbm(value):
    return pltpu.with_memory_space_constraint(value, pltpu.HBM)


def as_column(ref, k):
    row = jnp.concatenate([ref[s, k : k + 1, :].astype(F32) for s in range(ref.shape[0])], axis=1)
    return jnp.transpose(jnp.broadcast_to(row, (row.shape[1], row.shape[1])))[:, 0:1]


def pack_kernel(groups, owned, block, meta_ref, tokens_ref, route_ref, *refs):
    sends, (select_ref, pick_ref, share, sem) = refs[: groups - 1], refs[groups - 1 :]
    rows, cols = share.shape
    steps = rows // block
    lanes = pl.ds(pl.multiple_of(meta_ref[meta_ref.shape[0] - 1] * cols, cols), cols)
    copies = [
        pltpu.make_async_copy(tokens_ref.at[s, :, lanes], share.at[pl.ds(s * block, block)], sem.at[s])
        for s in range(steps)
    ]
    for copy in copies:
        copy.start()
    per_expert = steps * CAP
    per_group = owned * per_expert
    slots = groups * per_group
    token = lax.broadcasted_iota(jnp.int32, (rows, rows), 0)
    lane = lax.broadcasted_iota(jnp.int32, (rows, rows), 1)
    before = jnp.where((lane < token) & (lane // block == token // block), 1.0, 0.0).astype(BF16)
    named = [as_column(route_ref, k) for k in range(2)]
    lane = lane.astype(F32)
    member = jnp.where((lane == named[0]) | (lane == named[1]), 1.0, 0.0).astype(BF16)
    earlier = jnp.dot(before, member, preferred_element_type=F32)
    slot = lax.broadcasted_iota(jnp.int32, (rows, slots), 1)
    step = lax.broadcasted_iota(jnp.int32, (rows, slots), 0) // block
    group = (meta_ref[0] + slot // per_group) % groups
    expert = (group * owned + slot % per_group // per_expert).astype(F32)
    here = slot % per_expert // CAP == step
    spot = (slot % CAP).astype(F32)
    total = jnp.zeros((rows, slots), F32)
    for k in range(2):
        position = jnp.sum(jnp.where(lane == named[k], earlier, 0.0), axis=1, keepdims=True)
        pick = jnp.where((expert == named[k]) & here & (spot == position), 1.0, 0.0)
        pick_ref[k] = pick.astype(BF16)
        total = total + pick
    select = jnp.transpose(total).astype(BF16)
    select_ref[...] = select[:per_group]
    for copy in copies:
        copy.wait()
    for k in range(1, groups):
        sends[k - 1][...] = jnp.dot(
            select[k * per_group : (k + 1) * per_group], share[...], preferred_element_type=F32
        ).astype(BF16)


def pack_slots(meta, tokens, route, groups, owned, cols):
    steps, block, width = tokens.shape
    rows = steps * block
    per_group = owned * steps * CAP
    vmem = pl.BlockSpec(memory_space=pltpu.VMEM)
    return pl.pallas_call(
        functools.partial(pack_kernel, groups, owned, block),
        grid_spec=pltpu.PrefetchScalarGridSpec(
            num_scalar_prefetch=1,
            grid=(),
            in_specs=[pl.BlockSpec(memory_space=pltpu.HBM), vmem],
            out_specs=[vmem] * (groups + 1),
            scratch_shapes=[pltpu.VMEM((rows, cols), BF16), pltpu.SemaphoreType.DMA((steps,))],
        ),
        out_shape=[jax.ShapeDtypeStruct((per_group, cols), BF16)] * (groups - 1)
        + [
            jax.ShapeDtypeStruct((per_group, rows), BF16),
            jax.ShapeDtypeStruct((2, rows, groups * per_group), BF16),
        ],
        compiler_params=pltpu.CompilerParams(vmem_limit_bytes=SMALL_VMEM),
        cost_estimate=pl.CostEstimate(flops=10**7, bytes_accessed=4 * rows * cols, transcendentals=0),
        name="pack_slots",
    )(meta, in_hbm(tokens), route.transpose(0, 2, 1))


def own_kernel(select_ref, tokens_ref, out_ref):
    every = jnp.concatenate([tokens_ref[s] for s in range(tokens_ref.shape[0])], axis=0)
    out_ref[...] = jnp.dot(select_ref[...], every, preferred_element_type=F32).astype(BF16)


def own_slots(select, tokens):
    vmem = pl.BlockSpec(memory_space=pltpu.VMEM)
    return pl.pallas_call(
        own_kernel,
        in_specs=[vmem, vmem],
        out_specs=vmem,
        out_shape=jax.ShapeDtypeStruct((select.shape[0], tokens.shape[2]), BF16),
        compiler_params=pltpu.CompilerParams(vmem_limit_bytes=SMALL_VMEM),
        cost_estimate=pl.CostEstimate(flops=10**8, bytes_accessed=4 * tokens.size, transcendentals=0),
        name="own_slots",
    )(select, tokens)


def combine_kernel(pick_ref, weight_ref, *refs):
    out_ref = refs[-1]
    steps, block, _ = out_ref.shape
    rows = jnp.concatenate([ref[...] for ref in refs[:-1]], axis=0)
    total = jnp.zeros((steps * block, out_ref.shape[2]), F32)
    for k in range(2):
        total = total + as_column(weight_ref, k) * jnp.dot(pick_ref[k], rows, preferred_element_type=F32)
    for s in range(steps):
        out_ref[s] = total[s * block : (s + 1) * block].astype(BF16)


def combine_slots(pick, weight, parts):
    steps, block, _ = weight.shape
    cols = parts[0].shape[1]
    vmem = pl.BlockSpec(memory_space=pltpu.VMEM)
    return pl.pallas_call(
        combine_kernel,
        in_specs=[vmem] * (2 + len(parts)),
        out_specs=vmem,
        out_shape=jax.ShapeDtypeStruct((steps, block, cols), BF16),
        compiler_params=pltpu.CompilerParams(vmem_limit_bytes=SMALL_VMEM),
        cost_estimate=pl.CostEstimate(flops=10**7, bytes_accessed=10**6, transcendentals=0),
        name="combine_slots",
    )(pick, weight.transpose(0, 2, 1), *parts)


def delta_kernel(groups, meta_ref, list_ref, count_ref, first_ref, second_ref, grad_ref, *refs):
    outs, (first_buf, second_buf, grad_buf, sem) = refs[:groups], refs[groups:]
    owned = outs[0].shape[0]

    def copies(at, entry):
        expert = lax.rem(meta_ref[0] + at // owned, groups) * owned + at % owned
        block = list_ref[expert, entry]
        rows = pl.ds(pl.multiple_of(block * BLOCK_ROWS, BLOCK_ROWS), BLOCK_ROWS)
        pair = pl.ds(pl.multiple_of(block // 2 * (2 * BLOCK_ROWS), 2 * BLOCK_ROWS), 2 * BLOCK_ROWS)
        return (
            pltpu.make_async_copy(first_ref.at[expert, rows, :], first_buf.at[at, entry], sem.at[0, at, entry]),
            pltpu.make_async_copy(second_ref.at[expert, rows, :], second_buf.at[at, entry], sem.at[1, at, entry]),
            pltpu.make_async_copy(grad_ref.at[expert, pair, :], grad_buf.at[at, entry], sem.at[2, at, entry]),
        )

    order = [(k % groups) * owned + e for k in range(1, groups + 1) for e in range(owned)]
    for at in order:
        for entry in range(MAXCH):
            for copy in copies(at, entry):
                copy.start()
    for at in order:
        expert = lax.rem(meta_ref[0] + at // owned, groups) * owned + at % owned
        parts = []
        for entry in range(MAXCH):
            for copy in copies(at, entry):
                copy.wait()
            odd = list_ref[expert, entry] % 2 == 1
            grads = grad_buf[at, entry].astype(F32)
            grad = jnp.where(odd, grads[BLOCK_ROWS:], grads[:BLOCK_ROWS])
            first = BETA_ONE * first_buf[at, entry] + (1.0 - BETA_ONE) * grad
            second = BETA_TWO * second_buf[at, entry] + (1.0 - BETA_TWO) * grad * grad
            step = LEARN_RATE * (first / FIRST_FIX) / (jnp.sqrt(second / SECOND_FIX) + ADAM_EPS)
            parts.append(jnp.where(entry < count_ref[expert], -step, 0.0))
        outs[at // owned][at % owned] = jnp.concatenate(parts, axis=0).astype(BF16)


def listed_deltas(meta, adam_first, adam_second, gradient, block_list, block_count, groups):
    experts, _, cols = adam_first.shape
    hbm = pl.BlockSpec(memory_space=pltpu.HBM)
    return pl.pallas_call(
        functools.partial(delta_kernel, groups),
        grid_spec=pltpu.PrefetchScalarGridSpec(
            num_scalar_prefetch=3,
            grid=(),
            in_specs=[hbm, hbm, hbm],
            out_specs=[pl.BlockSpec(memory_space=pltpu.VMEM)] * groups,
            scratch_shapes=[
                pltpu.VMEM((experts, MAXCH, BLOCK_ROWS, cols), F32),
                pltpu.VMEM((experts, MAXCH, BLOCK_ROWS, cols), F32),
                pltpu.VMEM((experts, MAXCH, 2 * BLOCK_ROWS, cols), BF16),
                pltpu.SemaphoreType.DMA((3, experts, MAXCH)),
            ],
        ),
        out_shape=[jax.ShapeDtypeStruct((experts // groups, MAXCH * BLOCK_ROWS, cols), BF16)] * groups,
        compiler_params=pltpu.CompilerParams(vmem_limit_bytes=SMALL_VMEM),
        cost_estimate=pl.CostEstimate(flops=10**6, bytes_accessed=experts * MAXCH * 96 * cols, transcendentals=0),
        name="listed_deltas",
    )(meta, block_list, block_count, in_hbm(adam_first), in_hbm(adam_second), in_hbm(gradient))


def adam_kernel(first_ref, second_ref, grad_ref, *refs):
    first_out, second_out = refs[-2:]
    grad = grad_ref[...].astype(F32)
    first_out[...] = BETA_ONE * first_ref[...] + (1.0 - BETA_ONE) * grad
    second_out[...] = BETA_TWO * second_ref[...] + (1.0 - BETA_TWO) * grad * grad


def adam_part(adam_first, adam_second, gradient, begin, end, filled=(), cost=None):
    _, rows, cols = adam_first.shape
    block = pl.BlockSpec((1, rows, cols), lambda e: (begin + e, 0, 0))
    size = (end - begin) * rows * cols
    return pl.pallas_call(
        adam_kernel,
        grid=(end - begin,),
        in_specs=[block, block, block] + [pl.BlockSpec(memory_space=pltpu.HBM)] * len(filled),
        out_specs=[block, block],
        out_shape=[jax.ShapeDtypeStruct(adam_first.shape, F32)] * 2,
        input_output_aliases={3 + i: i for i in range(len(filled))},
        compiler_params=pltpu.CompilerParams(vmem_limit_bytes=SMALL_VMEM),
        cost_estimate=cost or pl.CostEstimate(flops=8 * size, bytes_accessed=18 * size, transcendentals=0),
        name="adam_moments",
    )(in_hbm(adam_first), in_hbm(adam_second), in_hbm(gradient), *filled)


def gate_up_kernel(begin, shares, across, within, tile, first, last, meta_ref, own_ref, *refs):
    recv = [refs[i * within : (i + 1) * within] for i in range(shares)]
    gate_up_ref, refs = refs[shares * within], refs[shares * within + 1 :]
    sums_ref, refs = (None, refs) if first else (refs[0], refs[1:])
    out_ref, rows_ref, buf, sem = refs
    _, owned, slots, depth = rows_ref.shape
    ring = buf.shape[0]
    units = gate_up_ref.shape[3]
    cols = recv[0][0].shape[2]
    per_expert = own_ref.shape[0] // owned
    groups = slots // per_expert
    work = [
        (e, at, side, i)
        for e in range(owned)
        for at in range(0, units, tile)
        for side in range(2)
        for i in range(shares)
    ]

    def fetch(n):
        e, at, side, i = work[n]
        deep = pl.ds(pl.multiple_of(meta_ref[1 + begin + i] * depth, depth), depth)
        source = gate_up_ref.at[e, side, deep, pl.ds(at, tile)]
        return pltpu.make_async_copy(source, buf.at[n % ring], sem.at[n % ring])

    for n in range(min(ring, len(work))):
        fetch(n).start()
    for i in range(shares):
        for q in range(within):
            place = meta_ref[1 + across + q]
            start = (meta_ref[1 + begin + i] * within + place) * cols
            lanes = pl.ds(pl.multiple_of(start, cols), cols)
            into = pl.ds(pl.multiple_of(place * cols, cols), cols)
            for e in range(owned):
                mine = slice(e * per_expert, (e + 1) * per_expert)
                rows_ref[i, e, 0:per_expert, into] = own_ref[mine, lanes]
                for k in range(1, groups):
                    rows_ref[i, e, k * per_expert : (k + 1) * per_expert, into] = recv[i][q][k - 1, mine, :]
    total = gate = None
    for n, (e, at, side, i) in enumerate(work):
        fetch(n).wait()
        product = jnp.dot(rows_ref[i, e], buf[n % ring], preferred_element_type=F32)
        total = product if i == 0 else total + product
        if n + ring < len(work):
            fetch(n + ring).start()
        if i < shares - 1:
            continue
        if not first:
            total = total + sums_ref[e, side, :, at : at + tile]
        if not last:
            out_ref[e, side, :, at : at + tile] = total
        elif side == 0:
            gate = total
        else:
            out_ref[e, :, at : at + tile] = (gate * jax.nn.sigmoid(gate) * total).astype(BF16)


def gate_up_stage(meta, begin, across, own, received, gate_up, sums, last):
    owned, _, width, units = gate_up.shape
    shares, within = len(received), len(received[0])
    depth = within * received[0][0].shape[2]
    slots = own.shape[0] // owned * (1 + received[0][0].shape[0])
    tile = min(UNIT_TILE, units)
    ring = min(RING, owned * 2 * shares * (units // tile))
    vmem = pl.BlockSpec(memory_space=pltpu.VMEM)
    first = sums is None
    if last:
        out_shape = jax.ShapeDtypeStruct((owned, slots, units), BF16)
    else:
        out_shape = jax.ShapeDtypeStruct((owned, 2, slots, units), F32)
    return pl.pallas_call(
        functools.partial(gate_up_kernel, begin, shares, across, within, tile, first, last),
        grid_spec=pltpu.PrefetchScalarGridSpec(
            num_scalar_prefetch=1,
            grid=(),
            in_specs=[vmem] * (1 + shares * within)
            + [pl.BlockSpec(memory_space=pltpu.HBM)]
            + ([] if first else [vmem]),
            out_specs=vmem,
            scratch_shapes=[
                pltpu.VMEM((shares, owned, slots, depth), BF16),
                pltpu.VMEM((ring, depth, tile), BF16),
                pltpu.SemaphoreType.DMA((ring,)),
            ],
        ),
        out_shape=out_shape,
        compiler_params=pltpu.CompilerParams(vmem_limit_bytes=STAGE_VMEM),
        cost_estimate=pl.CostEstimate(
            flops=4 * owned * slots * depth * units * shares,
            bytes_accessed=4 * owned * depth * units * shares,
            transcendentals=0,
        ),
        name="gate_up_stage",
    )(meta, own, *sum([list(r) for r in received], []), in_hbm(gate_up), *([] if first else [sums]))


def fetch_kernel(expert, down_ref, out_ref, sem):
    copy = pltpu.make_async_copy(down_ref.at[expert], out_ref, sem)
    copy.start()
    copy.wait()


def fetch_down(down_weight, expert):
    return pl.pallas_call(
        functools.partial(fetch_kernel, expert),
        in_specs=[pl.BlockSpec(memory_space=pltpu.HBM)],
        out_specs=pl.BlockSpec(memory_space=pltpu.VMEM),
        out_shape=pltpu.VMEM(down_weight.shape[1:], down_weight.dtype),
        scratch_shapes=[pltpu.SemaphoreType.DMA],
        compiler_params=pltpu.CompilerParams(vmem_limit_bytes=SMALL_VMEM),
        cost_estimate=SHORT,
        name="fetch_down",
    )(in_hbm(down_weight))


def patch_kernel(groups, owned, meta_ref, list_ref, *refs):
    deltas, downs, outs = refs[:groups], refs[groups : groups + owned], refs[groups + owned :]
    cols = deltas[0].shape[2]
    listed = MAXCH * BLOCK_ROWS
    span = BLOCK_ROWS * STRIDE
    row = lax.broadcasted_iota(jnp.int32, (MAXCH * span, listed), 0)
    col = lax.broadcasted_iota(jnp.int32, (MAXCH * span, listed), 1)
    spread = ((row // STRIDE == col) & (row % STRIDE == 0)).astype(F32).astype(BF16)
    for k in range(groups):
        source = lax.rem(meta_ref[0] - k + groups, groups)
        lanes = pl.ds(pl.multiple_of(source * cols, cols), cols)
        for e in range(owned):
            added = jnp.dot(spread, deltas[k][e], preferred_element_type=F32)
            for entry in range(MAXCH):
                block = list_ref[meta_ref[0] * owned + e, entry]
                where = pl.ds(pl.multiple_of(block * span, span), span)
                fresh = downs[e][where, lanes].astype(F32) + added[entry * span : (entry + 1) * span]
                outs[e][where, lanes] = fresh.astype(BF16)


def patch_down(meta, block_list, deltas, downs):
    groups, owned = len(deltas), len(downs)
    vmem = pl.BlockSpec(memory_space=pltpu.VMEM)
    return pl.pallas_call(
        functools.partial(patch_kernel, groups, owned),
        grid_spec=pltpu.PrefetchScalarGridSpec(
            num_scalar_prefetch=2, grid=(), in_specs=[vmem] * (groups + owned), out_specs=[vmem] * owned
        ),
        out_shape=[pltpu.VMEM(d.shape, d.dtype) for d in downs],
        input_output_aliases={2 + groups + e: e for e in range(owned)},
        compiler_params=pltpu.CompilerParams(vmem_limit_bytes=SMALL_VMEM),
        cost_estimate=SHORT,
        name="patch_down",
    )(meta, block_list, *deltas, *[pltpu.with_memory_space_constraint(d, pltpu.VMEM) for d in downs])


def down_kernel(share, across, within, per_expert, meta_ref, hidden_ref, *refs):
    owned, slots, _ = hidden_ref.shape
    downs, outs = refs[:owned], refs[owned:]
    rows, cols = outs[0].shape
    groups = slots // per_expert
    for q in list(range(1, within)) + [0]:
        first_col = (meta_ref[1 + share] * within + meta_ref[1 + across + q]) * cols
        lanes = pl.ds(pl.multiple_of(first_col, cols), cols)
        for e in range(owned):
            part = jnp.dot(hidden_ref[e], downs[e][:, lanes], preferred_element_type=F32).astype(BF16)
            for k in range(groups):
                at = (k * owned + e) * per_expert
                part_of = PIECES * at // rows
                into = outs[0] if q == 0 else outs[PIECES * (q - 1) + 1 + part_of]
                at = at if q == 0 else at - part_of * (rows // PIECES)
                into[at : at + per_expert, :] = part[k * per_expert : (k + 1) * per_expert]


def down_pieces(meta, share, across, within, per_expert, hidden, downs, cols):
    owned, slots, units = hidden.shape
    rows = owned * slots
    vmem = pl.BlockSpec(memory_space=pltpu.VMEM)
    return pl.pallas_call(
        functools.partial(down_kernel, share, across, within, per_expert),
        grid_spec=pltpu.PrefetchScalarGridSpec(
            num_scalar_prefetch=1,
            grid=(),
            in_specs=[vmem] * (1 + owned),
            out_specs=[vmem] * (1 + PIECES * (within - 1)),
        ),
        out_shape=[jax.ShapeDtypeStruct((rows, cols), BF16)]
        + [jax.ShapeDtypeStruct((rows // PIECES, cols), BF16)] * (PIECES * (within - 1)),
        compiler_params=pltpu.CompilerParams(vmem_limit_bytes=SMALL_VMEM),
        cost_estimate=pl.CostEstimate(
            flops=2 * owned * slots * units * cols * within,
            bytes_accessed=2 * owned * units * cols * within,
            transcendentals=0,
        ),
        name="down_mixed",
    )(meta, hidden, *downs)


def swap(value, axis, distance):
    return lax.ppermute(value, axis, [(i, i ^ distance) for i in range(lax.axis_size(axis))])


def shift(value, axis, distance):
    size = lax.axis_size(axis)
    return lax.ppermute(value, axis, [(i, (i + distance) % size) for i in range(size)])


def on_device(
    tokens,
    route,
    route_weight,
    gate_up,
    down_weight,
    adam_first,
    adam_second,
    gradient,
    block_list,
    block_count,
):
    groups = lax.axis_size("expert")
    across, within = lax.axis_size("fsdp"), lax.axis_size("tensor")
    at_z, at_f, at_t = lax.axis_index("expert"), lax.axis_index("fsdp"), lax.axis_index("tensor")
    owned = gate_up.shape[0]
    steps, block, width = tokens.shape
    cols = width // (across * within)
    lists = block_list.reshape(block_list.shape[0], MAXCH)
    counts = block_count.reshape(-1)

    meta = jnp.stack(
        [at_z]
        + [at_f ^ r for r in range(across)]
        + [at_t ^ q for q in range(within)]
        + [at_f * within + at_t]
    ).astype(jnp.int32)

    *sends, select, pick = pack_slots(meta, tokens, route, groups, owned, cols)
    arrived = [shift(send, "expert", k) for k, send in enumerate(sends, 1)]
    mine = own_slots(select, tokens)
    deltas = listed_deltas(meta, adam_first, adam_second, gradient, lists, counts, groups)
    down_source, deltas = lax.optimization_barrier((down_weight, deltas))
    downs = [fetch_down(down_source, 0)]
    arrived, deltas, mine, downs = lax.optimization_barrier((arrived, deltas, mine, downs))
    away = jnp.stack(arrived)
    early = {k: shift(deltas[k], "expert", k) for k in (1, groups - 1)}

    def stage(begin, columns, sums, last):
        received = [[c] + [swap(c, "tensor", q) for q in range(1, within)] for c in columns]
        return gate_up_stage(meta, begin, across, mine, received, gate_up, sums, last)

    others = [swap(away, "fsdp", r) for r in range(1, across)]
    sums = stage(0, [away], None, False)
    experts = adam_first.shape[0]
    parts_at = (experts // 4, experts // 4 + experts * 3 // 8, experts)
    adam_in = (adam_first, adam_second, gradient)
    adam_in, down_source, deltas, early, sums = lax.optimization_barrier(
        (adam_in, down_source, deltas, early, sums)
    )
    late = {k: shift(deltas[k], "expert", k) for k in range(2, groups - 1)}
    filled = adam_part(*adam_in, 0, parts_at[0], cost=SHORT)
    downs = downs + [fetch_down(down_source, e) for e in range(1, owned)]
    downs = patch_down(meta, lists, [{0: deltas[0], **early, **late}[k] for k in range(groups)], downs)
    others, downs, filled, sums = lax.optimization_barrier((others, downs, filled, sums))
    hidden = stage(1, others, sums, True)

    def down(r, order):
        pieces = down_pieces(order, r, across, within, steps * CAP, hidden, downs, cols)
        return pieces[0], [swap(pieces[i], "tensor", (i - 1) // PIECES + 1) for i in range(1, len(pieces))]

    def add(*terms):
        total = terms[0].astype(F32)
        for term in terms[1:]:
            total = total + term.astype(F32)
        return total.astype(BF16)

    rows = groups * owned * steps * CAP

    def joined(pair):
        return [jnp.concatenate(pair[1][i : i + PIECES]) for i in range(0, len(pair[1]), PIECES)]

    def summed(pair, *more):
        return add(pair[0], *joined(pair), *more)

    far_sum = summed(down(across - 1, meta))
    if across == 4:
        far_up, far_low = far_sum[: rows // 2], far_sum[rows // 2 :]
        order, far_up, far_low = lax.optimization_barrier((meta, far_up, far_low))
        by_one, by_two = swap(far_up, "fsdp", 1), swap(far_low, "fsdp", 2)
        near = [down(r, order) for r in (1, 2)]
        by_one, by_two, near = lax.optimization_barrier((by_one, by_two, near))
        passed = [jnp.pad(by_two, ((rows // 2, 0), (0, 0))), jnp.pad(by_one, ((0, rows // 2), (0, 0)))]
        others = [swap(summed(near[i], passed[i]), "fsdp", i + 1) for i in range(2)]
    else:
        order, far_sum = lax.optimization_barrier((meta, far_sum))
        others = [swap(summed(down(r, order)), "fsdp", r) for r in range(1, across - 1)]
        others.append(swap(far_sum, "fsdp", across - 1))
    last = down(0, order)
    adam_in, filled, raw = lax.optimization_barrier((adam_in, filled, last[0]))
    filled = adam_part(*adam_in, parts_at[0], parts_at[1], filled)
    parts = add(raw, *joined(last), *others).reshape(groups, rows // groups, cols)
    adam_in, filled, parts = lax.optimization_barrier((adam_in, filled, parts))
    back = [shift(parts[k], "expert", -k) for k in range(1, groups)]
    first_new, second_new = adam_part(*adam_in, parts_at[1], parts_at[2], filled)
    return (combine_slots(pick, route_weight, [parts[0], *back]), first_new, second_new)


def solution(mesh):
    return jax.shard_map(
        on_device,
        mesh=mesh,
        in_specs=(
            P(None, "expert", None),
            P(None, "expert", None),
            P(None, "expert", None),
            P("expert", None, None, ("fsdp", "tensor")),
            P("expert", ("fsdp", "tensor"), None),
            P(None, ("fsdp", "tensor"), "expert"),
            P(None, ("fsdp", "tensor"), "expert"),
            P(None, ("fsdp", "tensor"), "expert"),
            P(None, ("fsdp", "tensor"), None),
            P(None, ("fsdp", "tensor")),
        ),
        out_specs=(
            P(None, "expert", ("fsdp", "tensor")),
            P(None, ("fsdp", "tensor"), "expert"),
            P(None, ("fsdp", "tensor"), "expert"),
        ),
        check_vma=False,
    )
```

```python
import functools

import jax
import jax.numpy as jnp
from jax import lax
from jax.experimental import pallas as pl
from jax.experimental.pallas import tpu as pltpu
from jax.sharding import PartitionSpec as P

STRIDE = 4
BLOCK_ROWS = 8
MAXCH = 4
CAP = 32
PIECES = 2
ADAM_ROWS = 128
RING = 12
UNIT_TILE = 512

BETA_ONE = 0.9
BETA_TWO = 0.95
LEARN_RATE = 0.03
ADAM_EPS = 1e-08
FIRST_FIX = 1.0 - 0.9**10
SECOND_FIX = 1.0 - 0.95**10

SHORT = pl.CostEstimate(flops=1, bytes_accessed=1, transcendentals=0)

F32 = jnp.float32
BF16 = jnp.bfloat16
SMALL_VMEM = 16 * 2**20
STAGE_VMEM = 24 * 2**20


def in_hbm(value):
    return pltpu.with_memory_space_constraint(value, pltpu.HBM)


def as_column(ref, k):
    row = jnp.concatenate([ref[s, k : k + 1, :].astype(F32) for s in range(ref.shape[0])], axis=1)
    return jnp.transpose(jnp.broadcast_to(row, (row.shape[1], row.shape[1])))[:, 0:1]


def pack_kernel(groups, owned, block, meta_ref, tokens_ref, route_ref, *refs):
    sends, (select_ref, pick_ref, share, sem) = refs[: groups - 1], refs[groups - 1 :]
    rows, cols = share.shape
    steps = rows // block
    lanes = pl.ds(pl.multiple_of(meta_ref[meta_ref.shape[0] - 1] * cols, cols), cols)
    copies = [
        pltpu.make_async_copy(tokens_ref.at[s, :, lanes], share.at[pl.ds(s * block, block)], sem.at[s])
        for s in range(steps)
    ]
    for copy in copies:
        copy.start()
    per_expert = steps * CAP
    per_group = owned * per_expert
    slots = groups * per_group
    token = lax.broadcasted_iota(jnp.int32, (rows, rows), 0)
    lane = lax.broadcasted_iota(jnp.int32, (rows, rows), 1)
    before = jnp.where((lane < token) & (lane // block == token // block), 1.0, 0.0).astype(BF16)
    named = [as_column(route_ref, k) for k in range(2)]
    lane = lane.astype(F32)
    member = jnp.where((lane == named[0]) | (lane == named[1]), 1.0, 0.0).astype(BF16)
    earlier = jnp.dot(before, member, preferred_element_type=F32)
    slot = lax.broadcasted_iota(jnp.int32, (rows, slots), 1)
    step = lax.broadcasted_iota(jnp.int32, (rows, slots), 0) // block
    group = (meta_ref[0] + slot // per_group) % groups
    expert = (group * owned + slot % per_group // per_expert).astype(F32)
    here = slot % per_expert // CAP == step
    spot = (slot % CAP).astype(F32)
    total = jnp.zeros((rows, slots), F32)
    for k in range(2):
        position = jnp.sum(jnp.where(lane == named[k], earlier, 0.0), axis=1, keepdims=True)
        pick = jnp.where((expert == named[k]) & here & (spot == position), 1.0, 0.0)
        pick_ref[k] = pick.astype(BF16)
        total = total + pick
    select = jnp.transpose(total).astype(BF16)
    select_ref[...] = select[:per_group]
    for copy in copies:
        copy.wait()
    for k in range(1, groups):
        sends[k - 1][...] = jnp.dot(
            select[k * per_group : (k + 1) * per_group], share[...], preferred_element_type=F32
        ).astype(BF16)


def pack_slots(meta, tokens, route, groups, owned, cols):
    steps, block, width = tokens.shape
    rows = steps * block
    per_group = owned * steps * CAP
    vmem = pl.BlockSpec(memory_space=pltpu.VMEM)
    return pl.pallas_call(
        functools.partial(pack_kernel, groups, owned, block),
        grid_spec=pltpu.PrefetchScalarGridSpec(
            num_scalar_prefetch=1,
            grid=(),
            in_specs=[pl.BlockSpec(memory_space=pltpu.HBM), vmem],
            out_specs=[vmem] * (groups + 1),
            scratch_shapes=[pltpu.VMEM((rows, cols), BF16), pltpu.SemaphoreType.DMA((steps,))],
        ),
        out_shape=[jax.ShapeDtypeStruct((per_group, cols), BF16)] * (groups - 1)
        + [
            jax.ShapeDtypeStruct((per_group, rows), BF16),
            jax.ShapeDtypeStruct((2, rows, groups * per_group), BF16),
        ],
        compiler_params=pltpu.CompilerParams(vmem_limit_bytes=SMALL_VMEM),
        cost_estimate=pl.CostEstimate(flops=10**7, bytes_accessed=4 * rows * cols, transcendentals=0),
        name="pack_slots",
    )(meta, in_hbm(tokens), route.transpose(0, 2, 1))


def own_kernel(select_ref, tokens_ref, out_ref):
    every = jnp.concatenate([tokens_ref[s] for s in range(tokens_ref.shape[0])], axis=0)
    out_ref[...] = jnp.dot(select_ref[...], every, preferred_element_type=F32).astype(BF16)


def own_slots(select, tokens):
    vmem = pl.BlockSpec(memory_space=pltpu.VMEM)
    return pl.pallas_call(
        own_kernel,
        in_specs=[vmem, vmem],
        out_specs=vmem,
        out_shape=jax.ShapeDtypeStruct((select.shape[0], tokens.shape[2]), BF16),
        compiler_params=pltpu.CompilerParams(vmem_limit_bytes=SMALL_VMEM),
        cost_estimate=pl.CostEstimate(flops=10**8, bytes_accessed=4 * tokens.size, transcendentals=0),
        name="own_slots",
    )(select, tokens)


def combine_kernel(pick_ref, weight_ref, *refs):
    out_ref = refs[-1]
    steps, block, _ = out_ref.shape
    rows = jnp.concatenate([ref[...] for ref in refs[:-1]], axis=0)
    total = jnp.zeros((steps * block, out_ref.shape[2]), F32)
    for k in range(2):
        total = total + as_column(weight_ref, k) * jnp.dot(pick_ref[k], rows, preferred_element_type=F32)
    for s in range(steps):
        out_ref[s] = total[s * block : (s + 1) * block].astype(BF16)


def combine_slots(pick, weight, parts):
    steps, block, _ = weight.shape
    cols = parts[0].shape[1]
    vmem = pl.BlockSpec(memory_space=pltpu.VMEM)
    return pl.pallas_call(
        combine_kernel,
        in_specs=[vmem] * (2 + len(parts)),
        out_specs=vmem,
        out_shape=jax.ShapeDtypeStruct((steps, block, cols), BF16),
        compiler_params=pltpu.CompilerParams(vmem_limit_bytes=SMALL_VMEM),
        cost_estimate=pl.CostEstimate(flops=10**7, bytes_accessed=10**6, transcendentals=0),
        name="combine_slots",
    )(pick, weight.transpose(0, 2, 1), *parts)


def delta_kernel(groups, meta_ref, list_ref, count_ref, first_ref, second_ref, grad_ref, *refs):
    outs, (first_buf, second_buf, grad_buf, sem) = refs[:groups], refs[groups:]
    owned = outs[0].shape[0]

    def copies(at, entry):
        expert = lax.rem(meta_ref[0] + at // owned, groups) * owned + at % owned
        block = list_ref[expert, entry]
        rows = pl.ds(pl.multiple_of(block * BLOCK_ROWS, BLOCK_ROWS), BLOCK_ROWS)
        pair = pl.ds(pl.multiple_of(block // 2 * (2 * BLOCK_ROWS), 2 * BLOCK_ROWS), 2 * BLOCK_ROWS)
        return (
            pltpu.make_async_copy(first_ref.at[expert, rows, :], first_buf.at[at, entry], sem.at[0, at, entry]),
            pltpu.make_async_copy(second_ref.at[expert, rows, :], second_buf.at[at, entry], sem.at[1, at, entry]),
            pltpu.make_async_copy(grad_ref.at[expert, pair, :], grad_buf.at[at, entry], sem.at[2, at, entry]),
        )

    order = [(k % groups) * owned + e for k in range(1, groups + 1) for e in range(owned)]
    for at in order:
        for entry in range(MAXCH):
            for copy in copies(at, entry):
                copy.start()
    for at in order:
        expert = lax.rem(meta_ref[0] + at // owned, groups) * owned + at % owned
        parts = []
        for entry in range(MAXCH):
            for copy in copies(at, entry):
                copy.wait()
            odd = list_ref[expert, entry] % 2 == 1
            grads = grad_buf[at, entry].astype(F32)
            grad = jnp.where(odd, grads[BLOCK_ROWS:], grads[:BLOCK_ROWS])
            first = BETA_ONE * first_buf[at, entry] + (1.0 - BETA_ONE) * grad
            second = BETA_TWO * second_buf[at, entry] + (1.0 - BETA_TWO) * grad * grad
            step = LEARN_RATE * (first / FIRST_FIX) / (jnp.sqrt(second / SECOND_FIX) + ADAM_EPS)
            parts.append(jnp.where(entry < count_ref[expert], -step, 0.0))
        outs[at // owned][at % owned] = jnp.concatenate(parts, axis=0).astype(BF16)


def listed_deltas(meta, adam_first, adam_second, gradient, block_list, block_count, groups):
    experts, _, cols = adam_first.shape
    hbm = pl.BlockSpec(memory_space=pltpu.HBM)
    return pl.pallas_call(
        functools.partial(delta_kernel, groups),
        grid_spec=pltpu.PrefetchScalarGridSpec(
            num_scalar_prefetch=3,
            grid=(),
            in_specs=[hbm, hbm, hbm],
            out_specs=[pl.BlockSpec(memory_space=pltpu.VMEM)] * groups,
            scratch_shapes=[
                pltpu.VMEM((experts, MAXCH, BLOCK_ROWS, cols), F32),
                pltpu.VMEM((experts, MAXCH, BLOCK_ROWS, cols), F32),
                pltpu.VMEM((experts, MAXCH, 2 * BLOCK_ROWS, cols), BF16),
                pltpu.SemaphoreType.DMA((3, experts, MAXCH)),
            ],
        ),
        out_shape=[jax.ShapeDtypeStruct((experts // groups, MAXCH * BLOCK_ROWS, cols), BF16)] * groups,
        compiler_params=pltpu.CompilerParams(vmem_limit_bytes=SMALL_VMEM),
        cost_estimate=pl.CostEstimate(flops=10**6, bytes_accessed=experts * MAXCH * 96 * cols, transcendentals=0),
        name="listed_deltas",
    )(meta, block_list, block_count, in_hbm(adam_first), in_hbm(adam_second), in_hbm(gradient))


def adam_kernel(first_ref, second_ref, grad_ref, *refs):
    first_out, second_out = refs[-2:]
    grad = grad_ref[...].astype(F32)
    first_out[...] = BETA_ONE * first_ref[...] + (1.0 - BETA_ONE) * grad
    second_out[...] = BETA_TWO * second_ref[...] + (1.0 - BETA_TWO) * grad * grad


def adam_part(adam_first, adam_second, gradient, begin, end, filled=(), cost=None):
    _, rows, cols = adam_first.shape
    lines = min(ADAM_ROWS, rows)
    block = pl.BlockSpec((1, lines, cols), lambda e, j: (begin + e, j, 0))
    size = (end - begin) * rows * cols
    return pl.pallas_call(
        adam_kernel,
        grid=(end - begin, rows // lines),
        in_specs=[block, block, block] + [pl.BlockSpec(memory_space=pltpu.HBM)] * len(filled),
        out_specs=[block, block],
        out_shape=[jax.ShapeDtypeStruct(adam_first.shape, F32)] * 2,
        input_output_aliases={3 + i: i for i in range(len(filled))},
        compiler_params=pltpu.CompilerParams(vmem_limit_bytes=SMALL_VMEM),
        cost_estimate=cost or pl.CostEstimate(flops=8 * size, bytes_accessed=18 * size, transcendentals=0),
        name="adam_moments",
    )(in_hbm(adam_first), in_hbm(adam_second), in_hbm(gradient), *filled)


def gate_up_kernel(begin, shares, across, within, tile, first, last, meta_ref, own_ref, *refs):
    recv = [refs[i * within : (i + 1) * within] for i in range(shares)]
    gate_up_ref, refs = refs[shares * within], refs[shares * within + 1 :]
    sums_ref, refs = (None, refs) if first else (refs[0], refs[1:])
    out_ref, rows_ref, buf, sem = refs
    _, owned, slots, depth = rows_ref.shape
    ring = buf.shape[0]
    units = gate_up_ref.shape[3]
    cols = recv[0][0].shape[2]
    per_expert = own_ref.shape[0] // owned
    groups = slots // per_expert
    work = [
        (e, at, side, i)
        for e in range(owned)
        for at in range(0, units, tile)
        for side in range(2)
        for i in range(shares)
    ]

    def fetch(n):
        e, at, side, i = work[n]
        deep = pl.ds(pl.multiple_of(meta_ref[1 + begin + i] * depth, depth), depth)
        source = gate_up_ref.at[e, side, deep, pl.ds(at, tile)]
        return pltpu.make_async_copy(source, buf.at[n % ring], sem.at[n % ring])

    for n in range(min(ring, len(work))):
        fetch(n).start()
    for i in range(shares):
        for q in range(within):
            place = meta_ref[1 + across + q]
            start = (meta_ref[1 + begin + i] * within + place) * cols
            lanes = pl.ds(pl.multiple_of(start, cols), cols)
            into = pl.ds(pl.multiple_of(place * cols, cols), cols)
            for e in range(owned):
                mine = slice(e * per_expert, (e + 1) * per_expert)
                rows_ref[i, e, 0:per_expert, into] = own_ref[mine, lanes]
                for k in range(1, groups):
                    rows_ref[i, e, k * per_expert : (k + 1) * per_expert, into] = recv[i][q][k - 1, mine, :]
    total = gate = None
    for n, (e, at, side, i) in enumerate(work):
        fetch(n).wait()
        product = jnp.dot(rows_ref[i, e], buf[n % ring], preferred_element_type=F32)
        total = product if i == 0 else total + product
        if n + ring < len(work):
            fetch(n + ring).start()
        if i < shares - 1:
            continue
        if not first:
            total = total + sums_ref[e, side, :, at : at + tile]
        if not last:
            out_ref[e, side, :, at : at + tile] = total
        elif side == 0:
            gate = total
        else:
            out_ref[e, :, at : at + tile] = (gate * jax.nn.sigmoid(gate) * total).astype(BF16)


def gate_up_stage(meta, begin, across, own, received, gate_up, sums, last):
    owned, _, width, units = gate_up.shape
    shares, within = len(received), len(received[0])
    depth = within * received[0][0].shape[2]
    slots = own.shape[0] // owned * (1 + received[0][0].shape[0])
    tile = min(UNIT_TILE, units)
    ring = min(RING, owned * 2 * shares * (units // tile))
    vmem = pl.BlockSpec(memory_space=pltpu.VMEM)
    first = sums is None
    if last:
        out_shape = jax.ShapeDtypeStruct((owned, slots, units), BF16)
    else:
        out_shape = jax.ShapeDtypeStruct((owned, 2, slots, units), F32)
    return pl.pallas_call(
        functools.partial(gate_up_kernel, begin, shares, across, within, tile, first, last),
        grid_spec=pltpu.PrefetchScalarGridSpec(
            num_scalar_prefetch=1,
            grid=(),
            in_specs=[vmem] * (1 + shares * within)
            + [pl.BlockSpec(memory_space=pltpu.HBM)]
            + ([] if first else [vmem]),
            out_specs=vmem,
            scratch_shapes=[
                pltpu.VMEM((shares, owned, slots, depth), BF16),
                pltpu.VMEM((ring, depth, tile), BF16),
                pltpu.SemaphoreType.DMA((ring,)),
            ],
        ),
        out_shape=out_shape,
        compiler_params=pltpu.CompilerParams(vmem_limit_bytes=STAGE_VMEM),
        cost_estimate=pl.CostEstimate(
            flops=4 * owned * slots * depth * units * shares,
            bytes_accessed=4 * owned * depth * units * shares,
            transcendentals=0,
        ),
        name="gate_up_stage",
    )(meta, own, *sum([list(r) for r in received], []), in_hbm(gate_up), *([] if first else [sums]))


def fetch_kernel(expert, down_ref, out_ref, sem):
    copy = pltpu.make_async_copy(down_ref.at[expert], out_ref, sem)
    copy.start()
    copy.wait()


def fetch_down(down_weight, expert):
    return pl.pallas_call(
        functools.partial(fetch_kernel, expert),
        in_specs=[pl.BlockSpec(memory_space=pltpu.HBM)],
        out_specs=pl.BlockSpec(memory_space=pltpu.VMEM),
        out_shape=pltpu.VMEM(down_weight.shape[1:], down_weight.dtype),
        scratch_shapes=[pltpu.SemaphoreType.DMA],
        compiler_params=pltpu.CompilerParams(vmem_limit_bytes=SMALL_VMEM),
        cost_estimate=SHORT,
        name="fetch_down",
    )(in_hbm(down_weight))


def patch_kernel(groups, owned, meta_ref, list_ref, *refs):
    deltas, downs, outs = refs[:groups], refs[groups : groups + owned], refs[groups + owned :]
    cols = deltas[0].shape[2]
    listed = MAXCH * BLOCK_ROWS
    span = BLOCK_ROWS * STRIDE
    row = lax.broadcasted_iota(jnp.int32, (MAXCH * span, listed), 0)
    col = lax.broadcasted_iota(jnp.int32, (MAXCH * span, listed), 1)
    spread = ((row // STRIDE == col) & (row % STRIDE == 0)).astype(F32).astype(BF16)
    for k in range(groups):
        source = lax.rem(meta_ref[0] - k + groups, groups)
        lanes = pl.ds(pl.multiple_of(source * cols, cols), cols)
        for e in range(owned):
            added = jnp.dot(spread, deltas[k][e], preferred_element_type=F32)
            for entry in range(MAXCH):
                block = list_ref[meta_ref[0] * owned + e, entry]
                where = pl.ds(pl.multiple_of(block * span, span), span)
                fresh = downs[e][where, lanes].astype(F32) + added[entry * span : (entry + 1) * span]
                outs[e][where, lanes] = fresh.astype(BF16)


def patch_down(meta, block_list, deltas, downs):
    groups, owned = len(deltas), len(downs)
    vmem = pl.BlockSpec(memory_space=pltpu.VMEM)
    return pl.pallas_call(
        functools.partial(patch_kernel, groups, owned),
        grid_spec=pltpu.PrefetchScalarGridSpec(
            num_scalar_prefetch=2, grid=(), in_specs=[vmem] * (groups + owned), out_specs=[vmem] * owned
        ),
        out_shape=[pltpu.VMEM(d.shape, d.dtype) for d in downs],
        input_output_aliases={2 + groups + e: e for e in range(owned)},
        compiler_params=pltpu.CompilerParams(vmem_limit_bytes=SMALL_VMEM),
        cost_estimate=SHORT,
        name="patch_down",
    )(meta, block_list, *deltas, *[pltpu.with_memory_space_constraint(d, pltpu.VMEM) for d in downs])


def down_kernel(share, across, within, per_expert, meta_ref, hidden_ref, *refs):
    owned, slots, _ = hidden_ref.shape
    downs, outs = refs[:owned], refs[owned:]
    rows, cols = outs[0].shape
    groups = slots // per_expert
    for q in list(range(1, within)) + [0]:
        first_col = (meta_ref[1 + share] * within + meta_ref[1 + across + q]) * cols
        lanes = pl.ds(pl.multiple_of(first_col, cols), cols)
        for e in range(owned):
            part = jnp.dot(hidden_ref[e], downs[e][:, lanes], preferred_element_type=F32).astype(BF16)
            for k in range(groups):
                at = (k * owned + e) * per_expert
                part_of = PIECES * at // rows
                into = outs[0] if q == 0 else outs[PIECES * (q - 1) + 1 + part_of]
                at = at if q == 0 else at - part_of * (rows // PIECES)
                into[at : at + per_expert, :] = part[k * per_expert : (k + 1) * per_expert]


def down_pieces(meta, share, across, within, per_expert, hidden, downs, cols):
    owned, slots, units = hidden.shape
    rows = owned * slots
    vmem = pl.BlockSpec(memory_space=pltpu.VMEM)
    return pl.pallas_call(
        functools.partial(down_kernel, share, across, within, per_expert),
        grid_spec=pltpu.PrefetchScalarGridSpec(
            num_scalar_prefetch=1,
            grid=(),
            in_specs=[vmem] * (1 + owned),
            out_specs=[vmem] * (1 + PIECES * (within - 1)),
        ),
        out_shape=[jax.ShapeDtypeStruct((rows, cols), BF16)]
        + [jax.ShapeDtypeStruct((rows // PIECES, cols), BF16)] * (PIECES * (within - 1)),
        compiler_params=pltpu.CompilerParams(vmem_limit_bytes=SMALL_VMEM),
        cost_estimate=pl.CostEstimate(
            flops=2 * owned * slots * units * cols * within,
            bytes_accessed=2 * owned * units * cols * within,
            transcendentals=0,
        ),
        name="down_mixed",
    )(meta, hidden, *downs)


def swap(value, axis, distance):
    return lax.ppermute(value, axis, [(i, i ^ distance) for i in range(lax.axis_size(axis))])


def shift(value, axis, distance):
    size = lax.axis_size(axis)
    return lax.ppermute(value, axis, [(i, (i + distance) % size) for i in range(size)])


def on_device(
    tokens,
    route,
    route_weight,
    gate_up,
    down_weight,
    adam_first,
    adam_second,
    gradient,
    block_list,
    block_count,
):
    groups = lax.axis_size("expert")
    across, within = lax.axis_size("fsdp"), lax.axis_size("tensor")
    at_z, at_f, at_t = lax.axis_index("expert"), lax.axis_index("fsdp"), lax.axis_index("tensor")
    owned = gate_up.shape[0]
    steps, block, width = tokens.shape
    cols = width // (across * within)
    lists = block_list.reshape(block_list.shape[0], MAXCH)
    counts = block_count.reshape(-1)

    meta = jnp.stack(
        [at_z]
        + [at_f ^ r for r in range(across)]
        + [at_t ^ q for q in range(within)]
        + [at_f * within + at_t]
    ).astype(jnp.int32)

    *sends, select, pick = pack_slots(meta, tokens, route, groups, owned, cols)
    arrived = [shift(send, "expert", k) for k, send in enumerate(sends, 1)]
    mine = own_slots(select, tokens)
    deltas = listed_deltas(meta, adam_first, adam_second, gradient, lists, counts, groups)
    down_source, deltas = lax.optimization_barrier((down_weight, deltas))
    downs = [fetch_down(down_source, 0)]
    arrived, deltas, mine, downs = lax.optimization_barrier((arrived, deltas, mine, downs))
    away = jnp.stack(arrived)
    early = {k: shift(deltas[k], "expert", k) for k in (1, groups - 1)}

    def stage(begin, received, sums, last):
        return gate_up_stage(meta, begin, across, mine, received, gate_up, sums, last)

    def with_other_cores(columns):
        return [columns] + [swap(columns, "tensor", q) for q in range(1, within)]

    others = [swap(away, "fsdp", r) for r in range(1, across)]
    sums = stage(0, [with_other_cores(away)], None, False)
    experts = adam_first.shape[0]
    parts_at = (experts // 8, experts * 5 // 8, experts)
    adam_in = (adam_first, adam_second, gradient)
    adam_in, down_source, deltas, early, sums = lax.optimization_barrier(
        (adam_in, down_source, deltas, early, sums)
    )
    late = {k: shift(deltas[k], "expert", k) for k in range(2, groups - 1)}
    filled = adam_part(*adam_in, 0, parts_at[0], cost=SHORT)
    downs = downs + [fetch_down(down_source, e) for e in range(1, owned)]
    near, downs = lax.optimization_barrier((others[:-1], downs))
    near = [with_other_cores(columns) for columns in near]
    downs = patch_down(meta, lists, [{0: deltas[0], **early, **late}[k] for k in range(groups)], downs)
    far, downs, filled, sums = lax.optimization_barrier((others[-1], downs, filled, sums))
    hidden = stage(1, near + [with_other_cores(far)], sums, True)

    def down(r, order):
        pieces = down_pieces(order, r, across, within, steps * CAP, hidden, downs, cols)
        return pieces[0], [swap(pieces[i], "tensor", (i - 1) // PIECES + 1) for i in range(1, len(pieces))]

    def add(*terms):
        total = terms[0].astype(F32)
        for term in terms[1:]:
            total = total + term.astype(F32)
        return total.astype(BF16)

    rows = groups * owned * steps * CAP

    def joined(pair):
        return [jnp.concatenate(pair[1][i : i + PIECES]) for i in range(0, len(pair[1]), PIECES)]

    def summed(pair, *more):
        return add(pair[0], *joined(pair), *more)

    far_sum = summed(down(across - 1, meta))
    if across == 4:
        far_up, far_low = far_sum[: rows // 2], far_sum[rows // 2 :]
        order, far_up, far_low = lax.optimization_barrier((meta, far_up, far_low))
        by_one, by_two = swap(far_up, "fsdp", 1), swap(far_low, "fsdp", 2)
        near = [down(r, order) for r in (1, 2)]
        by_one, by_two, near = lax.optimization_barrier((by_one, by_two, near))
        passed = [jnp.pad(by_two, ((rows // 2, 0), (0, 0))), jnp.pad(by_one, ((0, rows // 2), (0, 0)))]
        others = [swap(summed(near[i], passed[i]), "fsdp", i + 1) for i in range(2)]
    else:
        order, far_sum = lax.optimization_barrier((meta, far_sum))
        others = [swap(summed(down(r, order)), "fsdp", r) for r in range(1, across - 1)]
        others.append(swap(far_sum, "fsdp", across - 1))
    last = down(0, order)
    adam_in, filled, raw = lax.optimization_barrier((adam_in, filled, last[0]))
    filled = adam_part(*adam_in, parts_at[0], parts_at[1], filled)
    parts = add(raw, *joined(last), *others).reshape(groups, rows // groups, cols)
    adam_in, filled, parts = lax.optimization_barrier((adam_in, filled, parts))
    back = [shift(parts[k], "expert", -k) for k in range(1, groups)]
    first_new, second_new = adam_part(*adam_in, parts_at[1], parts_at[2], filled)
    return (combine_slots(pick, route_weight, [parts[0], *back]), first_new, second_new)


def solution(mesh):
    return jax.shard_map(
        on_device,
        mesh=mesh,
        in_specs=(
            P(None, "expert", None),
            P(None, "expert", None),
            P(None, "expert", None),
            P("expert", None, None, ("fsdp", "tensor")),
            P("expert", ("fsdp", "tensor"), None),
            P(None, ("fsdp", "tensor"), "expert"),
            P(None, ("fsdp", "tensor"), "expert"),
            P(None, ("fsdp", "tensor"), "expert"),
            P(None, ("fsdp", "tensor"), None),
            P(None, ("fsdp", "tensor")),
        ),
        out_specs=(
            P(None, "expert", ("fsdp", "tensor")),
            P(None, ("fsdp", "tensor"), "expert"),
            P(None, ("fsdp", "tensor"), "expert"),
        ),
        check_vma=False,
    )
```

```python
import functools

import jax
import jax.numpy as jnp
from jax import lax
from jax.experimental import pallas as pl
from jax.experimental.pallas import tpu as pltpu
from jax.sharding import PartitionSpec as P

STRIDE = 4
BLOCK_ROWS = 8
MAXCH = 4
CAP = 32
PIECES = 2
ADAM_ROWS = 256
RING = 12
UNIT_TILE = 512

BETA_ONE = 0.9
BETA_TWO = 0.95
LEARN_RATE = 0.03
ADAM_EPS = 1e-08
FIRST_FIX = 1.0 - 0.9**10
SECOND_FIX = 1.0 - 0.95**10

SHORT = pl.CostEstimate(flops=1, bytes_accessed=1, transcendentals=0)

F32 = jnp.float32
BF16 = jnp.bfloat16
SMALL_VMEM = 16 * 2**20
STAGE_VMEM = 24 * 2**20


def in_hbm(value):
    return pltpu.with_memory_space_constraint(value, pltpu.HBM)


def as_column(ref, k):
    row = jnp.concatenate([ref[s, k : k + 1, :].astype(F32) for s in range(ref.shape[0])], axis=1)
    return jnp.transpose(jnp.broadcast_to(row, (row.shape[1], row.shape[1])))[:, 0:1]


def pack_kernel(groups, owned, block, meta_ref, tokens_ref, route_ref, *refs):
    sends, (select_ref, pick_ref, share, sem) = refs[: groups - 1], refs[groups - 1 :]
    rows, cols = share.shape
    steps = rows // block
    lanes = pl.ds(pl.multiple_of(meta_ref[meta_ref.shape[0] - 1] * cols, cols), cols)
    copies = [
        pltpu.make_async_copy(tokens_ref.at[s, :, lanes], share.at[pl.ds(s * block, block)], sem.at[s])
        for s in range(steps)
    ]
    for copy in copies:
        copy.start()
    per_expert = steps * CAP
    per_group = owned * per_expert
    slots = groups * per_group
    token = lax.broadcasted_iota(jnp.int32, (rows, rows), 0)
    lane = lax.broadcasted_iota(jnp.int32, (rows, rows), 1)
    before = jnp.where((lane < token) & (lane // block == token // block), 1.0, 0.0).astype(BF16)
    named = [as_column(route_ref, k) for k in range(2)]
    lane = lane.astype(F32)
    member = jnp.where((lane == named[0]) | (lane == named[1]), 1.0, 0.0).astype(BF16)
    earlier = jnp.dot(before, member, preferred_element_type=F32)
    slot = lax.broadcasted_iota(jnp.int32, (rows, slots), 1)
    step = lax.broadcasted_iota(jnp.int32, (rows, slots), 0) // block
    group = (meta_ref[0] + slot // per_group) % groups
    expert = (group * owned + slot % per_group // per_expert).astype(F32)
    here = slot % per_expert // CAP == step
    spot = (slot % CAP).astype(F32)
    total = jnp.zeros((rows, slots), F32)
    for k in range(2):
        position = jnp.sum(jnp.where(lane == named[k], earlier, 0.0), axis=1, keepdims=True)
        pick = jnp.where((expert == named[k]) & here & (spot == position), 1.0, 0.0)
        pick_ref[k] = pick.astype(BF16)
        total = total + pick
    select = jnp.transpose(total).astype(BF16)
    select_ref[...] = select[:per_group]
    for copy in copies:
        copy.wait()
    for k in range(1, groups):
        sends[k - 1][...] = jnp.dot(
            select[k * per_group : (k + 1) * per_group], share[...], preferred_element_type=F32
        ).astype(BF16)


def pack_slots(meta, tokens, route, groups, owned, cols):
    steps, block, width = tokens.shape
    rows = steps * block
    per_group = owned * steps * CAP
    vmem = pl.BlockSpec(memory_space=pltpu.VMEM)
    return pl.pallas_call(
        functools.partial(pack_kernel, groups, owned, block),
        grid_spec=pltpu.PrefetchScalarGridSpec(
            num_scalar_prefetch=1,
            grid=(),
            in_specs=[pl.BlockSpec(memory_space=pltpu.HBM), vmem],
            out_specs=[vmem] * (groups + 1),
            scratch_shapes=[pltpu.VMEM((rows, cols), BF16), pltpu.SemaphoreType.DMA((steps,))],
        ),
        out_shape=[jax.ShapeDtypeStruct((per_group, cols), BF16)] * (groups - 1)
        + [
            jax.ShapeDtypeStruct((per_group, rows), BF16),
            jax.ShapeDtypeStruct((2, rows, groups * per_group), BF16),
        ],
        compiler_params=pltpu.CompilerParams(vmem_limit_bytes=SMALL_VMEM),
        cost_estimate=pl.CostEstimate(flops=10**7, bytes_accessed=4 * rows * cols, transcendentals=0),
        name="pack_slots",
    )(meta, in_hbm(tokens), route.transpose(0, 2, 1))


def own_kernel(select_ref, tokens_ref, out_ref):
    every = jnp.concatenate([tokens_ref[s] for s in range(tokens_ref.shape[0])], axis=0)
    out_ref[...] = jnp.dot(select_ref[...], every, preferred_element_type=F32).astype(BF16)


def own_slots(select, tokens):
    vmem = pl.BlockSpec(memory_space=pltpu.VMEM)
    return pl.pallas_call(
        own_kernel,
        in_specs=[vmem, vmem],
        out_specs=vmem,
        out_shape=jax.ShapeDtypeStruct((select.shape[0], tokens.shape[2]), BF16),
        compiler_params=pltpu.CompilerParams(vmem_limit_bytes=SMALL_VMEM),
        cost_estimate=pl.CostEstimate(flops=10**8, bytes_accessed=4 * tokens.size, transcendentals=0),
        name="own_slots",
    )(select, tokens)


def combine_kernel(pick_ref, weight_ref, *refs):
    out_ref = refs[-1]
    steps, block, _ = out_ref.shape
    rows = jnp.concatenate([ref[...] for ref in refs[:-1]], axis=0)
    total = jnp.zeros((steps * block, out_ref.shape[2]), F32)
    for k in range(2):
        total = total + as_column(weight_ref, k) * jnp.dot(pick_ref[k], rows, preferred_element_type=F32)
    for s in range(steps):
        out_ref[s] = total[s * block : (s + 1) * block].astype(BF16)


def combine_slots(pick, weight, parts):
    steps, block, _ = weight.shape
    cols = parts[0].shape[1]
    vmem = pl.BlockSpec(memory_space=pltpu.VMEM)
    return pl.pallas_call(
        combine_kernel,
        in_specs=[vmem] * (2 + len(parts)),
        out_specs=vmem,
        out_shape=jax.ShapeDtypeStruct((steps, block, cols), BF16),
        compiler_params=pltpu.CompilerParams(vmem_limit_bytes=SMALL_VMEM),
        cost_estimate=pl.CostEstimate(flops=10**7, bytes_accessed=10**6, transcendentals=0),
        name="combine_slots",
    )(pick, weight.transpose(0, 2, 1), *parts)


def delta_kernel(groups, meta_ref, list_ref, count_ref, first_ref, second_ref, grad_ref, *refs):
    outs, (first_buf, second_buf, grad_buf, sem) = refs[:groups], refs[groups:]
    owned = outs[0].shape[0]

    def copies(at, entry):
        expert = lax.rem(meta_ref[0] + at // owned, groups) * owned + at % owned
        block = list_ref[expert, entry]
        rows = pl.ds(pl.multiple_of(block * BLOCK_ROWS, BLOCK_ROWS), BLOCK_ROWS)
        pair = pl.ds(pl.multiple_of(block // 2 * (2 * BLOCK_ROWS), 2 * BLOCK_ROWS), 2 * BLOCK_ROWS)
        return (
            pltpu.make_async_copy(first_ref.at[expert, rows, :], first_buf.at[at, entry], sem.at[0, at, entry]),
            pltpu.make_async_copy(second_ref.at[expert, rows, :], second_buf.at[at, entry], sem.at[1, at, entry]),
            pltpu.make_async_copy(grad_ref.at[expert, pair, :], grad_buf.at[at, entry], sem.at[2, at, entry]),
        )

    order = [(k % groups) * owned + e for k in range(1, groups + 1) for e in range(owned)]
    for at in order:
        for entry in range(MAXCH):
            for copy in copies(at, entry):
                copy.start()
    for at in order:
        expert = lax.rem(meta_ref[0] + at // owned, groups) * owned + at % owned
        parts = []
        for entry in range(MAXCH):
            for copy in copies(at, entry):
                copy.wait()
            odd = list_ref[expert, entry] % 2 == 1
            grads = grad_buf[at, entry].astype(F32)
            grad = jnp.where(odd, grads[BLOCK_ROWS:], grads[:BLOCK_ROWS])
            first = BETA_ONE * first_buf[at, entry] + (1.0 - BETA_ONE) * grad
            second = BETA_TWO * second_buf[at, entry] + (1.0 - BETA_TWO) * grad * grad
            step = LEARN_RATE * (first / FIRST_FIX) / (jnp.sqrt(second / SECOND_FIX) + ADAM_EPS)
            parts.append(jnp.where(entry < count_ref[expert], -step, 0.0))
        outs[at // owned][at % owned] = jnp.concatenate(parts, axis=0).astype(BF16)


def listed_deltas(meta, adam_first, adam_second, gradient, block_list, block_count, groups):
    experts, _, cols = adam_first.shape
    hbm = pl.BlockSpec(memory_space=pltpu.HBM)
    return pl.pallas_call(
        functools.partial(delta_kernel, groups),
        grid_spec=pltpu.PrefetchScalarGridSpec(
            num_scalar_prefetch=3,
            grid=(),
            in_specs=[hbm, hbm, hbm],
            out_specs=[pl.BlockSpec(memory_space=pltpu.VMEM)] * groups,
            scratch_shapes=[
                pltpu.VMEM((experts, MAXCH, BLOCK_ROWS, cols), F32),
                pltpu.VMEM((experts, MAXCH, BLOCK_ROWS, cols), F32),
                pltpu.VMEM((experts, MAXCH, 2 * BLOCK_ROWS, cols), BF16),
                pltpu.SemaphoreType.DMA((3, experts, MAXCH)),
            ],
        ),
        out_shape=[jax.ShapeDtypeStruct((experts // groups, MAXCH * BLOCK_ROWS, cols), BF16)] * groups,
        compiler_params=pltpu.CompilerParams(vmem_limit_bytes=SMALL_VMEM),
        cost_estimate=pl.CostEstimate(flops=10**6, bytes_accessed=experts * MAXCH * 96 * cols, transcendentals=0),
        name="listed_deltas",
    )(meta, block_list, block_count, in_hbm(adam_first), in_hbm(adam_second), in_hbm(gradient))


def adam_kernel(first_ref, second_ref, grad_ref, *refs):
    first_out, second_out = refs[-2:]
    grad = grad_ref[...].astype(F32)
    first_out[...] = BETA_ONE * first_ref[...] + (1.0 - BETA_ONE) * grad
    second_out[...] = BETA_TWO * second_ref[...] + (1.0 - BETA_TWO) * grad * grad


def adam_part(adam_first, adam_second, gradient, begin, end, filled=(), cost=None):
    _, rows, cols = adam_first.shape
    lines = min(ADAM_ROWS, rows)
    block = pl.BlockSpec((1, lines, cols), lambda e, j: (begin + e, j, 0))
    size = (end - begin) * rows * cols
    return pl.pallas_call(
        adam_kernel,
        grid=(end - begin, rows // lines),
        in_specs=[block, block, block] + [pl.BlockSpec(memory_space=pltpu.HBM)] * len(filled),
        out_specs=[block, block],
        out_shape=[jax.ShapeDtypeStruct(adam_first.shape, F32)] * 2,
        input_output_aliases={3 + i: i for i in range(len(filled))},
        compiler_params=pltpu.CompilerParams(vmem_limit_bytes=SMALL_VMEM),
        cost_estimate=cost or pl.CostEstimate(flops=8 * size, bytes_accessed=18 * size, transcendentals=0),
        name="adam_moments",
    )(in_hbm(adam_first), in_hbm(adam_second), in_hbm(gradient), *filled)


def gate_up_kernel(begin, shares, across, within, tile, first, last, meta_ref, own_ref, *refs):
    recv = [refs[i * within : (i + 1) * within] for i in range(shares)]
    gate_up_ref, refs = refs[shares * within], refs[shares * within + 1 :]
    sums_ref, refs = (None, refs) if first else (refs[0], refs[1:])
    out_ref, rows_ref, buf, sem = refs
    _, owned, slots, depth = rows_ref.shape
    ring = buf.shape[0]
    units = gate_up_ref.shape[3]
    cols = recv[0][0].shape[2]
    per_expert = own_ref.shape[0] // owned
    groups = slots // per_expert
    work = [
        (e, at, side, i)
        for e in range(owned)
        for at in range(0, units, tile)
        for side in range(2)
        for i in range(shares)
    ]

    def fetch(n):
        e, at, side, i = work[n]
        deep = pl.ds(pl.multiple_of(meta_ref[1 + begin + i] * depth, depth), depth)
        source = gate_up_ref.at[e, side, deep, pl.ds(at, tile)]
        return pltpu.make_async_copy(source, buf.at[n % ring], sem.at[n % ring])

    for n in range(min(ring, len(work))):
        fetch(n).start()
    for i in range(shares):
        for q in range(within):
            place = meta_ref[1 + across + q]
            start = (meta_ref[1 + begin + i] * within + place) * cols
            lanes = pl.ds(pl.multiple_of(start, cols), cols)
            into = pl.ds(pl.multiple_of(place * cols, cols), cols)
            for e in range(owned):
                mine = slice(e * per_expert, (e + 1) * per_expert)
                rows_ref[i, e, 0:per_expert, into] = own_ref[mine, lanes]
                for k in range(1, groups):
                    rows_ref[i, e, k * per_expert : (k + 1) * per_expert, into] = recv[i][q][k - 1, mine, :]
    total = gate = None
    for n, (e, at, side, i) in enumerate(work):
        fetch(n).wait()
        product = jnp.dot(rows_ref[i, e], buf[n % ring], preferred_element_type=F32)
        total = product if i == 0 else total + product
        if n + ring < len(work):
            fetch(n + ring).start()
        if i < shares - 1:
            continue
        if not first:
            total = total + sums_ref[e, side, :, at : at + tile]
        if not last:
            out_ref[e, side, :, at : at + tile] = total
        elif side == 0:
            gate = total
        else:
            out_ref[e, :, at : at + tile] = (gate * jax.nn.sigmoid(gate) * total).astype(BF16)


def gate_up_stage(meta, begin, across, own, received, gate_up, sums, last):
    owned, _, width, units = gate_up.shape
    shares, within = len(received), len(received[0])
    depth = within * received[0][0].shape[2]
    slots = own.shape[0] // owned * (1 + received[0][0].shape[0])
    tile = min(UNIT_TILE, units)
    ring = min(RING, owned * 2 * shares * (units // tile))
    vmem = pl.BlockSpec(memory_space=pltpu.VMEM)
    first = sums is None
    if last:
        out_shape = jax.ShapeDtypeStruct((owned, slots, units), BF16)
    else:
        out_shape = jax.ShapeDtypeStruct((owned, 2, slots, units), F32)
    return pl.pallas_call(
        functools.partial(gate_up_kernel, begin, shares, across, within, tile, first, last),
        grid_spec=pltpu.PrefetchScalarGridSpec(
            num_scalar_prefetch=1,
            grid=(),
            in_specs=[vmem] * (1 + shares * within)
            + [pl.BlockSpec(memory_space=pltpu.HBM)]
            + ([] if first else [vmem]),
            out_specs=vmem,
            scratch_shapes=[
                pltpu.VMEM((shares, owned, slots, depth), BF16),
                pltpu.VMEM((ring, depth, tile), BF16),
                pltpu.SemaphoreType.DMA((ring,)),
            ],
        ),
        out_shape=out_shape,
        compiler_params=pltpu.CompilerParams(vmem_limit_bytes=STAGE_VMEM),
        cost_estimate=pl.CostEstimate(
            flops=4 * owned * slots * depth * units * shares,
            bytes_accessed=4 * owned * depth * units * shares,
            transcendentals=0,
        ),
        name="gate_up_stage",
    )(meta, own, *sum([list(r) for r in received], []), in_hbm(gate_up), *([] if first else [sums]))


def fetch_kernel(expert, down_ref, out_ref, sem):
    copy = pltpu.make_async_copy(down_ref.at[expert], out_ref, sem)
    copy.start()
    copy.wait()


def fetch_down(down_weight, expert):
    return pl.pallas_call(
        functools.partial(fetch_kernel, expert),
        in_specs=[pl.BlockSpec(memory_space=pltpu.HBM)],
        out_specs=pl.BlockSpec(memory_space=pltpu.VMEM),
        out_shape=pltpu.VMEM(down_weight.shape[1:], down_weight.dtype),
        scratch_shapes=[pltpu.SemaphoreType.DMA],
        compiler_params=pltpu.CompilerParams(vmem_limit_bytes=SMALL_VMEM),
        cost_estimate=SHORT,
        name="fetch_down",
    )(in_hbm(down_weight))


def patch_kernel(groups, owned, meta_ref, list_ref, *refs):
    deltas, downs, outs = refs[:groups], refs[groups : groups + owned], refs[groups + owned :]
    cols = deltas[0].shape[2]
    listed = MAXCH * BLOCK_ROWS
    span = BLOCK_ROWS * STRIDE
    row = lax.broadcasted_iota(jnp.int32, (MAXCH * span, listed), 0)
    col = lax.broadcasted_iota(jnp.int32, (MAXCH * span, listed), 1)
    spread = ((row // STRIDE == col) & (row % STRIDE == 0)).astype(F32).astype(BF16)
    for k in range(groups):
        source = lax.rem(meta_ref[0] - k + groups, groups)
        lanes = pl.ds(pl.multiple_of(source * cols, cols), cols)
        for e in range(owned):
            added = jnp.dot(spread, deltas[k][e], preferred_element_type=F32)
            for entry in range(MAXCH):
                block = list_ref[meta_ref[0] * owned + e, entry]
                where = pl.ds(pl.multiple_of(block * span, span), span)
                fresh = downs[e][where, lanes].astype(F32) + added[entry * span : (entry + 1) * span]
                outs[e][where, lanes] = fresh.astype(BF16)


def patch_down(meta, block_list, deltas, downs):
    groups, owned = len(deltas), len(downs)
    vmem = pl.BlockSpec(memory_space=pltpu.VMEM)
    return pl.pallas_call(
        functools.partial(patch_kernel, groups, owned),
        grid_spec=pltpu.PrefetchScalarGridSpec(
            num_scalar_prefetch=2, grid=(), in_specs=[vmem] * (groups + owned), out_specs=[vmem] * owned
        ),
        out_shape=[pltpu.VMEM(d.shape, d.dtype) for d in downs],
        input_output_aliases={2 + groups + e: e for e in range(owned)},
        compiler_params=pltpu.CompilerParams(vmem_limit_bytes=SMALL_VMEM),
        cost_estimate=SHORT,
        name="patch_down",
    )(meta, block_list, *deltas, *[pltpu.with_memory_space_constraint(d, pltpu.VMEM) for d in downs])


def down_kernel(share, across, within, per_expert, meta_ref, hidden_ref, *refs):
    owned, slots, _ = hidden_ref.shape
    downs, outs = refs[:owned], refs[owned:]
    rows, cols = outs[0].shape
    groups = slots // per_expert
    for q in list(range(1, within)) + [0]:
        first_col = (meta_ref[1 + share] * within + meta_ref[1 + across + q]) * cols
        lanes = pl.ds(pl.multiple_of(first_col, cols), cols)
        for e in range(owned):
            part = jnp.dot(hidden_ref[e], downs[e][:, lanes], preferred_element_type=F32).astype(BF16)
            for k in range(groups):
                at = (k * owned + e) * per_expert
                part_of = PIECES * at // rows
                into = outs[0] if q == 0 else outs[PIECES * (q - 1) + 1 + part_of]
                at = at if q == 0 else at - part_of * (rows // PIECES)
                into[at : at + per_expert, :] = part[k * per_expert : (k + 1) * per_expert]


def down_pieces(meta, share, across, within, per_expert, hidden, downs, cols):
    owned, slots, units = hidden.shape
    rows = owned * slots
    vmem = pl.BlockSpec(memory_space=pltpu.VMEM)
    return pl.pallas_call(
        functools.partial(down_kernel, share, across, within, per_expert),
        grid_spec=pltpu.PrefetchScalarGridSpec(
            num_scalar_prefetch=1,
            grid=(),
            in_specs=[vmem] * (1 + owned),
            out_specs=[vmem] * (1 + PIECES * (within - 1)),
        ),
        out_shape=[jax.ShapeDtypeStruct((rows, cols), BF16)]
        + [jax.ShapeDtypeStruct((rows // PIECES, cols), BF16)] * (PIECES * (within - 1)),
        compiler_params=pltpu.CompilerParams(vmem_limit_bytes=SMALL_VMEM),
        cost_estimate=pl.CostEstimate(
            flops=2 * owned * slots * units * cols * within,
            bytes_accessed=2 * owned * units * cols * within,
            transcendentals=0,
        ),
        name="down_mixed",
    )(meta, hidden, *downs)


def swap(value, axis, distance):
    return lax.ppermute(value, axis, [(i, i ^ distance) for i in range(lax.axis_size(axis))])


def shift(value, axis, distance):
    size = lax.axis_size(axis)
    return lax.ppermute(value, axis, [(i, (i + distance) % size) for i in range(size)])


def on_device(
    tokens,
    route,
    route_weight,
    gate_up,
    down_weight,
    adam_first,
    adam_second,
    gradient,
    block_list,
    block_count,
):
    groups = lax.axis_size("expert")
    across, within = lax.axis_size("fsdp"), lax.axis_size("tensor")
    at_z, at_f, at_t = lax.axis_index("expert"), lax.axis_index("fsdp"), lax.axis_index("tensor")
    owned = gate_up.shape[0]
    steps, block, width = tokens.shape
    cols = width // (across * within)
    lists = block_list.reshape(block_list.shape[0], MAXCH)
    counts = block_count.reshape(-1)

    meta = jnp.stack(
        [at_z]
        + [at_f ^ r for r in range(across)]
        + [at_t ^ q for q in range(within)]
        + [at_f * within + at_t]
    ).astype(jnp.int32)

    *sends, select, pick = pack_slots(meta, tokens, route, groups, owned, cols)
    arrived = [shift(send, "expert", k) for k, send in enumerate(sends, 1)]
    mine = own_slots(select, tokens)
    deltas = listed_deltas(meta, adam_first, adam_second, gradient, lists, counts, groups)
    down_source, deltas = lax.optimization_barrier((down_weight, deltas))
    downs = [fetch_down(down_source, 0)]
    arrived, deltas, mine, downs = lax.optimization_barrier((arrived, deltas, mine, downs))
    away = jnp.stack(arrived)
    early = {k: shift(deltas[k], "expert", k) for k in (1, groups - 1)}

    def stage(begin, received, sums, last):
        return gate_up_stage(meta, begin, across, mine, received, gate_up, sums, last)

    def with_other_cores(columns):
        return [columns] + [swap(columns, "tensor", q) for q in range(1, within)]

    others = [swap(away, "fsdp", r) for r in range(1, across)]
    sums = stage(0, [with_other_cores(away)], None, False)
    experts = adam_first.shape[0]
    parts_at = (experts // 8, experts * 5 // 8, experts)
    adam_in = (adam_first, adam_second, gradient)
    adam_in, down_source, deltas, early, sums = lax.optimization_barrier(
        (adam_in, down_source, deltas, early, sums)
    )
    late = {k: shift(deltas[k], "expert", k) for k in range(2, groups - 1)}
    filled = adam_part(*adam_in, 0, parts_at[0], cost=SHORT)
    downs = downs + [fetch_down(down_source, e) for e in range(1, owned)]
    near, downs = lax.optimization_barrier((others[:-1], downs))
    near = [with_other_cores(columns) for columns in near]
    downs = patch_down(meta, lists, [{0: deltas[0], **early, **late}[k] for k in range(groups)], downs)
    far, downs, filled, sums = lax.optimization_barrier((others[-1], downs, filled, sums))
    hidden = stage(1, near + [with_other_cores(far)], sums, True)

    def down(r, order):
        pieces = down_pieces(order, r, across, within, steps * CAP, hidden, downs, cols)
        return pieces[0], [swap(pieces[i], "tensor", (i - 1) // PIECES + 1) for i in range(1, len(pieces))]

    def add(*terms):
        total = terms[0].astype(F32)
        for term in terms[1:]:
            total = total + term.astype(F32)
        return total.astype(BF16)

    rows = groups * owned * steps * CAP

    def joined(pair):
        return [jnp.concatenate(pair[1][i : i + PIECES]) for i in range(0, len(pair[1]), PIECES)]

    def summed(pair, *more):
        return add(pair[0], *joined(pair), *more)

    far_sum = summed(down(across - 1, meta))
    if across == 4:
        far_up, far_low = far_sum[: rows // 2], far_sum[rows // 2 :]
        order, far_up, far_low = lax.optimization_barrier((meta, far_up, far_low))
        by_one, by_two = swap(far_up, "fsdp", 1), swap(far_low, "fsdp", 2)
        near = [down(r, order) for r in (1, 2)]
        by_one, by_two, near = lax.optimization_barrier((by_one, by_two, near))
        passed = [jnp.pad(by_two, ((rows // 2, 0), (0, 0))), jnp.pad(by_one, ((0, rows // 2), (0, 0)))]
        others = [swap(summed(near[i], passed[i]), "fsdp", i + 1) for i in range(2)]
    else:
        order, far_sum = lax.optimization_barrier((meta, far_sum))
        others = [swap(summed(down(r, order)), "fsdp", r) for r in range(1, across - 1)]
        others.append(swap(far_sum, "fsdp", across - 1))
    last = down(0, order)
    adam_in, filled, raw = lax.optimization_barrier((adam_in, filled, last[0]))
    filled = adam_part(*adam_in, parts_at[0], parts_at[1], filled)
    parts = add(raw, *joined(last), *others).reshape(groups, rows // groups, cols)
    adam_in, filled, parts = lax.optimization_barrier((adam_in, filled, parts))
    back = [shift(parts[k], "expert", -k) for k in range(1, groups)]
    first_new, second_new = adam_part(*adam_in, parts_at[1], parts_at[2], filled)
    return (combine_slots(pick, route_weight, [parts[0], *back]), first_new, second_new)


def solution(mesh):
    return jax.shard_map(
        on_device,
        mesh=mesh,
        in_specs=(
            P(None, "expert", None),
            P(None, "expert", None),
            P(None, "expert", None),
            P("expert", None, None, ("fsdp", "tensor")),
            P("expert", ("fsdp", "tensor"), None),
            P(None, ("fsdp", "tensor"), "expert"),
            P(None, ("fsdp", "tensor"), "expert"),
            P(None, ("fsdp", "tensor"), "expert"),
            P(None, ("fsdp", "tensor"), None),
            P(None, ("fsdp", "tensor")),
        ),
        out_specs=(
            P(None, "expert", ("fsdp", "tensor")),
            P(None, ("fsdp", "tensor"), "expert"),
            P(None, ("fsdp", "tensor"), "expert"),
        ),
        check_vma=False,
    )
```
